128 devices in a mesh: fam: 4 (over z), ctx: 32 (over x, y, core).
Axes of the slice: x: 4, y: 4, z: 4, core: 2. Of those that a mesh axis runs over, the one named last changes fastest.
Arguments:
- queries: bfloat16 [4, 16384, 1024], P('fam', 'ctx'), may hold values from -7 to 7
- key_rows: bfloat16 [4, 16384, 1024], P('fam', 'ctx'), may hold values from -4 to 4
- value_rows: bfloat16 [4, 16384, 1024], P('fam', 'ctx'), may hold values from -6 to 6
- cotangent: bfloat16 [4, 16384, 1024], P('fam', 'ctx'), may hold values from -6 to 6
- out_weight: bfloat16 [1024, 1024], replicated, may hold values from -0.1875 to 0.1875
- prot_blocks: int32 [4, 32], P('fam'), may hold values from 1 to 8, 128 in all within a row
- last_fill: int32 [4, 32], P('fam'), may hold values from 1 to 128
- memory_slots: int32 [4, 512], P('fam'), may hold values from 0 to 511
Outputs:
- query_grad: bfloat16 [4, 16384, 1024], P('fam', 'ctx')
- key_grad: bfloat16 [4, 16384, 1024], P('fam', 'ctx')
- value_grad: bfloat16 [4, 16384, 1024], P('fam', 'ctx')
- weight_grad: float32 [1024, 1024], replicated
The draws below stay inside these ranges and needn't reach their ends.
Inputs may be any that keep to these rules, and one draw needn't show every extreme that they name: `prot_blocks`: each family's protein lengths, in blocks, sum to 128, and the longest has exactly 8 blocks.
All inputs are finite; a program needn't handle non-finite values.
Results may differ from the reference program's by a relative error of at most 0.015.
Values may be sent and summed in bfloat16 or wider, within the bound.
A program may use at most 128 MiB of HBM per device.

```python
import math
import jax
import jax.numpy as jnp
import numpy as np
from jax import lax

D = 1024
HEADS = 16
HEAD_DIM = 64
W = 512
BLK = 128
MOST_BLK = 8
MEM_DEV = 16
TOK_DEV = 512
FAMS = 4
LEN = 16384
NBLK = 128
NPROT = 32
MEMS = 512


def paired_rows(key):
    shape = (FAMS, LEN, D)
    query_base = jnp.clip(jax.random.normal(jax.random.fold_in(key, 11), shape, jnp.float32), -4.0, 4.0)
    key_base = jnp.clip(jax.random.normal(jax.random.fold_in(key, 12), shape, jnp.float32), -4.0, 4.0)
    return (query_base, key_base)


def draw_queries(key, part):
    return paired_rows(key)[0].astype(jnp.bfloat16)


def draw_key_rows(key, part):
    return paired_rows(key)[1].astype(jnp.bfloat16)


def place_ends(drawn, own_key, smallest, largest):
    longest = drawn.shape.index(max(drawn.shape))
    spots = []
    for shift in (0, 1):
        where = [jax.random.randint(jax.random.fold_in(own_key, axis), (), 0, length) for axis, length in enumerate(drawn.shape)]
        where[longest] = (where[longest] + shift) % drawn.shape[longest]
        spots.append(tuple(where))
    return drawn.at[spots[0]].set(smallest).at[spots[1]].set(largest)


def level_of(key, extent, shards, least, largest):
    factor_of = 1.0
    for dim, blocks in shards:
        heights = jax.random.uniform(jax.random.fold_in(jax.random.fold_in(key, 6), dim), (blocks,), jnp.float32, least / len(shards), largest / len(shards))
        factor_of = factor_of * jnp.repeat(jnp.exp(heights), extent[dim] // blocks).reshape((-1,) + (1,) * (len(extent) - 1 - dim))
    return factor_of


def length_profile(count, total, bound, skew):
    loads = [(1 << 20) // math.isqrt(rank ** skew) + 1 for rank in range(2, count + 1)]
    rest, given = total - bound - (count - 1), [1] * (count - 1)
    while rest > 0:
        free = [i for i in range(count - 1) if given[i] < bound]
        mass, remaining = sum([loads[i] for i in free]), rest
        for i in free:
            extra = min(bound - given[i], max(1, remaining * loads[i] // mass), rest)
            given[i] = given[i] + extra
            rest = rest - extra
    return np.array([bound] + given)


def uneven(key, amount, total, reach, lean):
    if amount == 2:
        one = jax.random.randint(key, (), max(1, total - reach), min(reach, total - 1) + 1)
        return jnp.stack([one, total - one])
    tallies = jnp.asarray(length_profile(amount, total, reach, lean), jnp.int32)
    pairs = (amount - 1) // 2
    giver, receiver = tallies[1:1 + 2 * pairs:2], tallies[2:2 + 2 * pairs:2]
    margin = jnp.minimum(giver - 1, reach - receiver)
    moved = jax.random.randint(jax.random.fold_in(key, 1), (pairs,), 0, 1 << 20) % (margin + 1)
    tallies = tallies.at[1:1 + 2 * pairs:2].set(giver - moved).at[2:2 + 2 * pairs:2].set(receiver + moved)
    return tallies[jax.random.permutation(jax.random.fold_in(key, 2), amount)]


def centred(stream_key, shape, spread, bound, shards=(), kind=jnp.bfloat16):
    entries = spread * jax.random.normal(stream_key, shape, jnp.float32)
    if shards:
        entries = entries * level_of(stream_key, shape, shards, -0.22, 0.18)
    return jnp.clip(entries, -bound, bound).astype(kind)


def setup_inputs(seed: int = 0) -> dict:
    splits = jax.random.split(jax.random.key(seed), 9)
    queries = draw_queries(jax.random.fold_in(splits[8], 71), 0)
    key_rows = draw_key_rows(jax.random.fold_in(splits[8], 71), 0)
    value_rows = centred(splits[2], (FAMS, LEN, D), 1.0, 6.0, ((0, 4), (1, 32)))
    cotangent = centred(splits[3], (FAMS, LEN, D), 1.0, 6.0, ((0, 4), (1, 32)))
    out_weight = centred(splits[4], (D, D), D ** -0.5, 0.1875)
    prot_blocks = jax.vmap(lambda own: uneven(own, NPROT, NBLK, MOST_BLK, 2))(jax.random.split(splits[5], FAMS)).reshape((FAMS, NPROT)).astype(jnp.int32)
    last_fill = place_ends(jax.random.randint(splits[6], (FAMS, NPROT), 1, BLK + 1), jax.random.fold_in(splits[6], 1), 1, BLK).astype(jnp.int32)
    memory_slots = place_ends(jax.random.randint(splits[7], (FAMS, MEMS), 0, TOK_DEV), jax.random.fold_in(splits[7], 1), 0, TOK_DEV - 1).astype(jnp.int32)
    return dict(queries=queries, key_rows=key_rows, value_rows=value_rows, cotangent=cotangent, out_weight=out_weight, prot_blocks=prot_blocks, last_fill=last_fill, memory_slots=memory_slots)


NEG_FILL = -1e30


def protein_tables(prot_blocks, last_fill):
    prot_ends = jnp.cumsum(prot_blocks).astype(jnp.int32)
    starts = (prot_ends - prot_blocks).astype(jnp.int32)
    valid_len = ((prot_blocks - 1) * BLK + last_fill).astype(jnp.int32)
    return prot_ends, starts, valid_len


def token_info(positions, tables):
    prot_ends, starts, valid_len = tables
    prot_count = prot_ends.shape[0]
    block_ids = jnp.floor_divide(positions, BLK)
    protein = jnp.sum((block_ids[:, None] >= prot_ends[None, :]).astype(jnp.int32), axis=1).astype(jnp.int32)
    onehot = protein[:, None] == jnp.arange(prot_count, dtype=jnp.int32)[None, :]
    first_block = jnp.sum(jnp.where(onehot, starts[None, :], 0), axis=1).astype(jnp.int32)
    allowed = jnp.sum(jnp.where(onehot, valid_len[None, :], 0), axis=1).astype(jnp.int32)
    is_valid = (positions >= 0) & (protein < prot_count) & (positions - first_block * BLK < allowed)
    return protein, is_valid


def band_mask(query_pos, query_info, key_pos, key_info):
    return (query_info[1][:, None] & key_info[1][None, :]
            & (query_info[0][:, None] == key_info[0][None, :])
            & (key_pos[None, :] <= query_pos[:, None])
            & (query_pos[:, None] - key_pos[None, :] < W))


def attend(query_blk, grad_blk, key_blk, value_blk, live_mask):
    scale = HEAD_DIM ** -0.5
    query_f = query_blk.astype(jnp.float32)
    grad_f = grad_blk.astype(jnp.float32)
    key_f = key_blk.astype(jnp.float32)
    value_f = value_blk.astype(jnp.float32)
    scores = jnp.einsum('qhe,khe->hqk', query_f, key_f) * scale
    live = live_mask[None]
    shifted = jnp.where(live, scores, NEG_FILL)
    row_max = jnp.max(shifted, axis=-1, keepdims=True)
    expo = jnp.where(live, jnp.exp(shifted - row_max), 0.0)
    row_sum = jnp.maximum(jnp.sum(expo, axis=-1, keepdims=True), 1.0)
    attn_prob = expo / row_sum
    prob_half = attn_prob.astype(jnp.bfloat16)
    prob_back = prob_half.astype(jnp.float32)
    attended = jnp.einsum('hqk,khe->qhe', prob_back, value_f).astype(jnp.bfloat16)
    grad_prob = jnp.einsum('qhe,khe->hqk', grad_f, value_f)
    row_dot = jnp.sum(attn_prob * grad_prob, axis=-1, keepdims=True)
    grad_score = (attn_prob * (grad_prob - row_dot) * scale).astype(jnp.bfloat16).astype(jnp.float32)
    grad_query = jnp.einsum('hqk,khe->qhe', grad_score, key_f)
    grad_key = jnp.einsum('hqk,qhe->khe', grad_score, query_f)
    grad_value = jnp.einsum('hqk,qhe->khe', prob_back, grad_f)
    return attended, grad_query, grad_key, grad_value


def family_grads(query_all, key_all, value_all, grad_out, out_weight, prot_blocks, last_fill, slots):
    tables = protein_tables(prot_blocks, last_fill)
    positions = jnp.arange(LEN, dtype=jnp.int32)
    protein, is_valid = token_info(positions, tables)
    source = (jnp.arange(MEMS, dtype=jnp.int32) // MEM_DEV) * TOK_DEV + slots
    mem_prot = protein[source]
    mem_valid = is_valid[source]
    key_memory = key_all[source].reshape(MEMS, HEADS, HEAD_DIM)
    value_memory = value_all[source].reshape(MEMS, HEADS, HEAD_DIM)
    grad_attn = jnp.dot(grad_out, out_weight.T, preferred_element_type=jnp.float32).astype(jnp.bfloat16)
    padding = jnp.zeros((W, D), jnp.bfloat16)
    key_pad = jnp.concatenate([padding, key_all], axis=0)
    value_pad = jnp.concatenate([padding, value_all], axis=0)
    pad_pos = jnp.arange(LEN + W, dtype=jnp.int32) - W
    pad_prot, pad_valid = token_info(pad_pos, tables)

    def step(carry, block_num):
        band_kgrad, band_vgrad, mem_kgrad, mem_vgrad = carry
        row_start = block_num * W
        query_blk = lax.dynamic_slice_in_dim(query_all, row_start, W).reshape(W, HEADS, HEAD_DIM)
        grad_blk = lax.dynamic_slice_in_dim(grad_attn, row_start, W).reshape(W, HEADS, HEAD_DIM)
        key_band = lax.dynamic_slice_in_dim(key_pad, row_start, 2 * W).reshape(2 * W, HEADS, HEAD_DIM)
        value_band = lax.dynamic_slice_in_dim(value_pad, row_start, 2 * W).reshape(2 * W, HEADS, HEAD_DIM)
        query_pos = row_start + jnp.arange(W, dtype=jnp.int32)
        query_info = (lax.dynamic_slice_in_dim(protein, row_start, W), lax.dynamic_slice_in_dim(is_valid, row_start, W))
        key_pos = row_start - W + jnp.arange(2 * W, dtype=jnp.int32)
        key_info = (lax.dynamic_slice_in_dim(pad_prot, row_start, 2 * W), lax.dynamic_slice_in_dim(pad_valid, row_start, 2 * W))
        band = band_mask(query_pos, query_info, key_pos, key_info)
        memory = query_info[1][:, None] & mem_valid[None, :] & (mem_prot[None, :] < query_info[0][:, None])
        live_mask = jnp.concatenate([band, memory], axis=1)
        key_blk = jnp.concatenate([key_band, key_memory], axis=0)
        value_blk = jnp.concatenate([value_band, value_memory], axis=0)
        attended, grad_query, grad_key, grad_value = attend(query_blk, grad_blk, key_blk, value_blk, live_mask)
        old_k = lax.dynamic_slice_in_dim(band_kgrad, row_start, 2 * W)
        band_kgrad = lax.dynamic_update_slice_in_dim(band_kgrad, old_k + grad_key[:2 * W].reshape(2 * W, D), row_start, 0)
        old_v = lax.dynamic_slice_in_dim(band_vgrad, row_start, 2 * W)
        band_vgrad = lax.dynamic_update_slice_in_dim(band_vgrad, old_v + grad_value[:2 * W].reshape(2 * W, D), row_start, 0)
        mem_kgrad = mem_kgrad + grad_key[2 * W:].reshape(MEMS, D)
        mem_vgrad = mem_vgrad + grad_value[2 * W:].reshape(MEMS, D)
        return (band_kgrad, band_vgrad, mem_kgrad, mem_vgrad), (attended.reshape(W, D), grad_query.reshape(W, D))

    init = (jnp.zeros((LEN + W, D), jnp.float32), jnp.zeros((LEN + W, D), jnp.float32),
            jnp.zeros((MEMS, D), jnp.float32), jnp.zeros((MEMS, D), jnp.float32))
    carry, stacked = lax.scan(step, init, jnp.arange(LEN // W, dtype=jnp.int32))
    band_kgrad, band_vgrad, mem_kgrad, mem_vgrad = carry
    attended = stacked[0].reshape(LEN, D)
    query_grad = stacked[1].reshape(LEN, D)
    key_grad = band_kgrad[W:].at[source].add(mem_kgrad)
    value_grad = band_vgrad[W:].at[source].add(mem_vgrad)
    weight_part = jnp.dot(attended.T, grad_out, preferred_element_type=jnp.float32)
    return query_grad.astype(jnp.bfloat16), key_grad.astype(jnp.bfloat16), value_grad.astype(jnp.bfloat16), weight_part


def reference(queries, key_rows, value_rows, cotangent, out_weight, prot_blocks, last_fill, memory_slots):
    query_list = []
    key_list = []
    value_list = []
    weight_total = jnp.zeros((D, D), jnp.float32)
    for family in range(FAMS):
        query_grad, key_grad, value_grad, weight_part = family_grads(
            queries[family], key_rows[family], value_rows[family], cotangent[family], out_weight,
            prot_blocks[family], last_fill[family], memory_slots[family])
        query_list.append(query_grad)
        key_list.append(key_grad)
        value_list.append(value_grad)
        weight_total = weight_total + weight_part
    weight_grad = weight_total * (FAMS * LEN) ** -0.5
    return jnp.stack(query_list), jnp.stack(key_list), jnp.stack(value_list), weight_grad
```

```python
import functools
import jax, jax.numpy as jnp
from jax import lax
from jax.sharding import PartitionSpec as P
from jax.experimental import pallas as pl
from jax.experimental.pallas import tpu as pltpu
F32=jnp.float32; BF=jnp.bfloat16
NEG=-1e30
def nt(a,b): return lax.dot_general(a,b,(((1,),(1,)),((),())),preferred_element_type=F32)
def nn(a,b): return lax.dot_general(a,b,(((1,),(0,)),((),())),preferred_element_type=F32)
def tn(a,b): return lax.dot_general(a,b,(((0,),(0,)),((),())),preferred_element_type=F32)
def make(QB, VM=60):
  NB=512//QB; KB=512+QB
  def kernel(q_ref,k_ref,v_ref,hk_ref,hv_ref,mk_ref,mv_ref,cot_ref,w_ref,kb_ref,valid_ref,
             dq_ref,dk_ref,dv_ref,w_out, kx,vx,dkt,dvt,att_ref):
    p=pl.program_id(0)
    @pl.when(p==0)
    def _():
      kx[:,128:]=kb_ref[...]
      l2=lax.broadcasted_iota(jnp.int32,(1536,128),1)
      vx[:,128:]=jnp.where(l2<2,1.0,0.0).astype(BF)
    kx[0:512,:128]=hk_ref[...]; kx[512:1024,:128]=k_ref[...]; kx[1024:1536,:128]=mk_ref[...]
    vx[0:512,:128]=hv_ref[...]; vx[512:1024,:128]=v_ref[...]; vx[1024:1536,:128]=mv_ref[...]
    do=nt(cot_ref[...],w_ref[...]).astype(BF)
    dkt[...]=jnp.zeros_like(dkt); dvt[...]=jnp.zeros_like(dvt)
    lane=lax.broadcasted_iota(jnp.int32,(QB,128),1); lo=lane<64
    lane2=lax.broadcasted_iota(jnp.int32,(2*QB,128),1)
    row2=lax.broadcasted_iota(jnp.int32,(2*QB,128),0)
    rr=lax.broadcasted_iota(jnp.int32,(2*QB,QB),0); rr=jnp.where(rr>=QB,rr-QB,rr)
    cc=lax.broadcasted_iota(jnp.int32,(2*QB,QB),1)
    tri_far=cc>rr; tri_near=cc<=rr
    z=jnp.zeros((QB,128),BF)
    for b in range(NB):
      rows=slice(b*QB,(b+1)*QB); band=slice(b*QB,b*QB+KB); mem=slice(1024,1536)
      qp=q_ref[rows,:]*jnp.asarray(0.125,BF)
      qs=jnp.concatenate([jnp.where(lo,qp,z),jnp.where(lo,z,qp)],0)
      r2=jnp.where(row2>=QB,row2-QB,row2)+b*QB
      oh=jnp.where(lane2==r2//128,1.0,0.0).astype(BF)
      qa=jnp.concatenate([qs,oh],1)
      sb=nt(qa,kx[band,:]); sm=nt(qa,kx[mem,:])
      s0=jnp.where(tri_far,sb[:,:QB],NEG); s2=jnp.where(tri_near,sb[:,512:],NEG)
      if QB<512: parts=[s0,sb[:,QB:512],s2,sm]
      else: parts=[s0,s2,sm]
      s=jnp.concatenate(parts,1)
      m=jnp.max(s,axis=1,keepdims=True)
      e=jnp.exp(s-m).astype(BF)
      eb=e[:,:KB]; em=e[:,KB:]
      o=nn(eb,vx[band,:])+nn(em,vx[mem,:])
      vl=valid_ref[rows,:]; vl=jnp.concatenate([vl,vl],0)
      inv=vl/jnp.maximum(o[:,128:129],1.0)
      att=o[:,:128]*inv
      dop=do[rows,:]
      dos=jnp.concatenate([jnp.where(lo,dop,z),jnp.where(lo,z,dop)],0)
      dosf=dos.astype(F32)
      rd=jnp.sum(att*dosf,axis=1,keepdims=True)
      hi=rd.astype(BF).astype(F32)
      pat=jnp.where(lane2==0,-hi,jnp.where(lane2==1,hi-rd,0.0)).astype(BF)
      da=jnp.concatenate([dos,pat],1)
      dpb=nt(da,vx[band,:]); dpm=nt(da,vx[mem,:])
      dsb=(eb.astype(F32)*dpb).astype(BF); dsm=(em.astype(F32)*dpm).astype(BF)
      dqs=nn(dsb,kx[band,:128])+nn(dsm,kx[mem,:128])
      dqs=dqs*(inv*0.125)
      dq_ref[rows,:]=jnp.where(lo,dqs[:QB],dqs[QB:]).astype(BF)
      att_ref[rows,:]=jnp.where(lo,att[:QB],att[QB:]).astype(BF)
      qn=(qs.astype(F32)*inv).astype(BF); don=(dosf*inv).astype(BF)
      dkt[:,band]+=tn(qn,dsb); dkt[:,mem]+=tn(qn,dsm)
      dvt[:,band]+=tn(don,eb); dvt[:,mem]+=tn(don,em)
    dk_ref[...]=dkt[...].T
    dv_ref[...]=dvt[...].T
    w_out[...]=tn(att_ref[...],cot_ref[...])
  def call(q,k,v,hk,hv,mk,mv,cot,w,kb,valid):
    col=pl.BlockSpec((512,128),lambda p:(0,p))
    full=lambda s: pl.BlockSpec(s,lambda p:(0,0))
    return pl.pallas_call(kernel,grid=(8,),
      in_specs=[col]*7+[full((512,1024)),pl.BlockSpec((128,1024),lambda p:(p,0)),full((1536,128)),full((512,1))],
      out_specs=[col,pl.BlockSpec((1536,128),lambda p:(0,p)),pl.BlockSpec((1536,128),lambda p:(0,p)),pl.BlockSpec((128,1024),lambda p:(p,0))],
      out_shape=[jax.ShapeDtypeStruct((512,1024),BF),jax.ShapeDtypeStruct((1536,1024),F32),jax.ShapeDtypeStruct((1536,1024),F32),jax.ShapeDtypeStruct((1024,1024),F32)],
      scratch_shapes=[pltpu.VMEM((1536,256),BF),pltpu.VMEM((1536,256),BF),pltpu.VMEM((128,1536),F32),pltpu.VMEM((128,1536),F32),pltpu.VMEM((512,128),BF)],
      compiler_params=pltpu.CompilerParams(vmem_limit_bytes=VM*2**20),name='attn')(q,k,v,hk,hv,mk,mv,cot,w,kb,valid)
  return call


def protein_tables(prot_blocks, last_fill):
    count = prot_blocks.shape[0]
    index = jnp.arange(count, dtype=jnp.int32)
    ends = jnp.sum(jnp.where(index[None, :] <= index[:, None], prot_blocks[None, :], 0), axis=1)
    return ends, ends - prot_blocks, (prot_blocks - 1) * 128 + last_fill


def token_info(positions, tables):
    ends, starts, filled = tables
    block = jnp.floor_divide(positions, 128)
    protein = jnp.sum((block[:, None] >= ends[None, :]).astype(jnp.int32), axis=1)
    hit = protein[:, None] == jnp.arange(ends.shape[0], dtype=jnp.int32)[None, :]
    first = jnp.sum(jnp.where(hit, starts[None, :], 0), axis=1)
    limit = jnp.sum(jnp.where(hit, filled[None, :], 0), axis=1)
    return protein, (positions >= 0) & (positions - first * 128 < limit)


def per_device(queries, key_rows, value_rows, cotangent, out_weight, prot_blocks, last_fill, memory_slots):
    q, k, v, cot = queries[0], key_rows[0], value_rows[0], cotangent[0]
    tables = protein_tables(prot_blocks[0], last_fill[0])
    slots = memory_slots[0]
    me = lax.axis_index("ctx")
    base = me * 512
    ext = base - 512 + jnp.arange(1024, dtype=jnp.int32)
    source = jnp.arange(512, dtype=jnp.int32) // 16 * 512 + slots
    ext_prot, ext_ok = token_info(ext, tables)
    mem_prot, mem_ok = token_info(source, tables)
    block_prot = ext_prot[512::128]
    band = ext_ok[:, None] & (ext_prot[:, None] == block_prot[None, :])
    memory = mem_ok[:, None] & (mem_prot[:, None] < block_prot[None, :])
    seen = jnp.concatenate([band, memory], 0)
    bias = jnp.pad(jnp.where(seen, 0.0, NEG).astype(BF), ((0, 0), (0, 124)))
    valid = ext_ok[512:].astype(F32)[:, None]
    own = lax.dynamic_slice_in_dim(slots, me * 16, 16)
    pick = (own[:, None] == jnp.arange(512, dtype=jnp.int32)[None, :]).astype(BF)
    mk = lax.all_gather(nn(pick, k).astype(BF), "ctx", axis=0, tiled=True)
    mv = lax.all_gather(nn(pick, v).astype(BF), "ctx", axis=0, tiled=True)
    ahead = [(i, i + 1) for i in range(31)]
    back = [(i + 1, i) for i in range(31)]
    hk, hv = lax.ppermute((k, v), "ctx", ahead)
    dq, dk, dv, weight = make(256)(q, k, v, hk, hv, mk, mv, cot, out_weight, bias, valid)
    weight = lax.psum(weight, ("fam", "ctx")) * (4 * 16384) ** -0.5
    bk, bv = lax.ppermute((dk[:512].astype(BF), dv[:512].astype(BF)), "ctx", back)
    gk = lax.psum_scatter(dk[1024:].astype(BF), "ctx", scatter_dimension=0, tiled=True)
    gv = lax.psum_scatter(dv[1024:].astype(BF), "ctx", scatter_dimension=0, tiled=True)
    dk = dk[512:1024] + bk.astype(F32) + tn(pick, gk)
    dv = dv[512:1024] + bv.astype(F32) + tn(pick, gv)
    return dq[None], dk.astype(BF)[None], dv.astype(BF)[None], weight


def solution(mesh):
    row = P("fam", "ctx", None)
    fam = P("fam", None)
    return jax.shard_map(
        per_device,
        mesh=mesh,
        in_specs=(row, row, row, row, P(), fam, fam, fam),
        out_specs=(row, row, row, P()),
        check_vma=False,
    )
```

```python
import jax
import jax.numpy as jnp
from jax import lax
from jax.experimental import pallas as pl
from jax.experimental.pallas import tpu as pltpu
from jax.sharding import PartitionSpec as P

F32 = jnp.float32
BF = jnp.bfloat16
NEG = -1e30
QB = 256
BAND = 512 + QB
PAIRS = 8
MESH = pl.DeviceIdType.MESH


def nt(a, b):
    return lax.dot_general(a, b, (((1,), (1,)), ((), ())), preferred_element_type=F32)


def nn(a, b):
    return lax.dot_general(a, b, (((1,), (0,)), ((), ())), preferred_element_type=F32)


def tn(a, b):
    return lax.dot_general(a, b, (((0,), (0,)), ((), ())), preferred_element_type=F32)


def cols(p):
    return pl.ds(pl.multiple_of(p * 128, 128), 128)


def part(index, size):
    return pl.ds(pl.multiple_of(index * size, size), size)


def kernel(
    q_ref, k_ref, v_ref, cot_ref, w_ref, pick_ref, slots_ref, blocks_ref, fill_ref,
    dq_ref, dk_ref, dv_ref, wg_ref,
    kx, vx, dkt, dvt, att, do_all, vcol, own,
    mem, halo, bsend, brecv, mg, srecv, xs, xrecv, ys, yrecv,
    wb, w1, ws2, w2, ws3, w3, ws4, w4, f5, f6, f7, f8,
    agy_s, agy_r, agx_s, agx_r, ags_s, ags_r, hal_s, hal_r, bak_s, bak_r,
    ms_s, ms_r, mx_s, mx_r, my_s, my_r,
    s1_s, s1_r, s2_s, s2_r, s3_s, s3_r, s4_s, s4_r, s5_s, s5_r, s6_s, s6_r, s7_s, s7_r, s8_s, s8_r,
):
    z = lax.axis_index("fam")
    me = lax.axis_index("ctx")
    x = me // 8
    y = (me // 2) % 4
    core = me % 2

    def at(xx, yy, cc):
        return (z, xx * 8 + yy * 2 + cc)

    sib = at(x, y, 1 - core)
    nxt = (z, (me + 1) % 32)
    prv = (z, (me + 31) % 32)
    across = (z, (me + 31 + 2 * core) % 32)
    ypeer = [at(x, (y + d) % 4, core) for d in (1, 2, 3)]
    xpeer = [at((x + d) % 4, y, core) for d in (1, 2, 3)]
    zpeer = [((z + d) % 4, me) for d in (1, 2, 3)]

    def rc(src, dst, send, recv, device):
        return pltpu.make_async_remote_copy(
            src_ref=src, dst_ref=dst, send_sem=send, recv_sem=recv, device_id=device, device_id_type=MESH
        )

    def ag_y():
        rows = part(core * 16 + x * 4 + y, 16)
        ref = mem.at[:, :, rows]
        return [rc(ref, ref, agy_s.at[d], agy_r.at[d], ypeer[d]) for d in range(3)]

    def ag_x(p):
        ref = mem.at[p, :, part(core * 4 + x, 64)]
        return [rc(ref, ref, agx_s.at[p, d], agx_r.at[p, d], xpeer[d]) for d in range(3)]

    def ag_s(p):
        ref = mem.at[p, :, part(core, 256)]
        return [rc(ref, ref, ags_s.at[p], ags_r.at[p], sib)]

    def halo_fwd(p):
        return [
            rc(r.at[:, cols(p)], halo.at[p, i], hal_s.at[p, i], hal_r.at[p, i], nxt)
            for i, r in enumerate((k_ref, v_ref))
        ]

    def halo_back(p):
        return [rc(bsend.at[p], brecv.at[p], bak_s.at[p], bak_r.at[p], prv)]

    def mem_s(p):
        return [rc(mg.at[p, :, part(1 - core, 256)], srecv.at[p], ms_s.at[p], ms_r.at[p], sib)]

    def mem_x(p):
        return [
            rc(xs.at[p, :, part((x + d + 1) % 4, 64)], xrecv.at[p, d], mx_s.at[p, d], mx_r.at[p, d], xpeer[d])
            for d in range(3)
        ]

    def mem_y(p):
        return [
            rc(ys.at[p, :, part((y + d + 1) % 4, 16)], yrecv.at[p, d], my_s.at[p, d], my_r.at[p, d], ypeer[d])
            for d in range(3)
        ]

    def wt1(p):
        return [rc(wb.at[p, 1 - core], w1.at[p], s1_s.at[p], s1_r.at[p], sib)]

    def wt2(p):
        return [
            rc(ws2.at[p, part((z + d + 1) % 4, 32)], w2.at[p, d], s2_s.at[p, d], s2_r.at[p, d], zpeer[d])
            for d in range(3)
        ]

    def wt3(p):
        return [
            rc(ws3.at[p, (y + d + 1) % 4], w3.at[p, d], s3_s.at[p, d], s3_r.at[p, d], ypeer[d])
            for d in range(3)
        ]

    def wt4(p):
        return [
            rc(ws4.at[p, part((x + d + 1) % 4, 8)], w4.at[p, d], s4_s.at[p, d], s4_r.at[p, d], xpeer[d])
            for d in range(3)
        ]

    def wt5(p):
        ref = f5.at[p, part(x, 8)]
        return [rc(ref, ref, s5_s.at[p, d], s5_r.at[p, d], xpeer[d]) for d in range(3)]

    def wt6(p):
        ref = f6.at[p, y]
        return [rc(ref, ref, s6_s.at[p, d], s6_r.at[p, d], ypeer[d]) for d in range(3)]

    def wt7(p):
        ref = f7.at[p, part(z, 32)]
        return [rc(ref, ref, s7_s.at[p, d], s7_r.at[p, d], zpeer[d]) for d in range(3)]

    def wt8(p):
        return [rc(f7.at[p], f8.at[p], s8_s.at[p], s8_r.at[p], sib)]

    def start(copies):
        for c in copies:
            c.start()

    def wait(copies):
        for c in copies:
            c.wait()

    barrier = pltpu.get_barrier_semaphore()
    for device in [sib, across] + ypeer + xpeer + zpeer:
        pl.semaphore_signal(barrier, inc=1, device_id=device, device_id_type=MESH)
    mine = part(core * 16 + x * 4 + y, 16)
    pick = pick_ref[...]
    for i, r in enumerate((k_ref, v_ref)):
        for p in range(PAIRS):
            mem[p, i, mine, :] = nn(pick, r[:, p * 128 : p * 128 + 128]).astype(BF)
    pl.semaphore_wait(barrier, 11)
    start(ag_y())
    start(halo_fwd(0))
    start(halo_fwd(1))

    pos_band = me * 512 - 512 + lax.broadcasted_iota(jnp.int32, (1, 1024), 1)
    order = lax.broadcasted_iota(jnp.int32, (1, 512), 1) // 16
    holder = (order % 16) * 2 + order // 16
    pos = jnp.concatenate([pos_band, holder * 512 + slots_ref[...]], axis=1)
    block = (pos + 512) // 128 - 4
    prot = jnp.zeros((1, 1536), jnp.int32)
    limit = jnp.zeros((1, 1536), jnp.int32)
    first = jnp.int32(0)
    for i in range(32):
        size = blocks_ref[0, i]
        end = first + size
        inside = (block >= first) & (block < end)
        prot = jnp.where(inside, i, prot)
        limit = jnp.where(inside, (end - 1) * 128 + fill_ref[0, i], limit)
        first = end
    real = (pos >= 0) & (pos < limit)
    is_mem = lax.broadcasted_iota(jnp.int32, (1, 1536), 1) >= 1024
    rows8 = lax.broadcasted_iota(jnp.int32, (8, 1536), 0)
    table = jnp.where(rows8 == 4, jnp.where(real, 1.0, 0.0), 0.0)
    for a in range(4):
        mine_prot = prot[:, 512 + a * 128 : 513 + a * 128]
        seen = real & ((is_mem & (prot < mine_prot)) | (jnp.logical_not(is_mem) & (prot == mine_prot)))
        table = jnp.where(rows8 == a, jnp.where(seen, 0.0, NEG), table)
    wide = jnp.concatenate([table, jnp.zeros((120, 1536), F32)], axis=0).T
    kx[:, 128:] = wide.astype(BF)
    vcol[...] = wide[512:1024, :]
    vx[:, 128:] = jnp.where(lax.broadcasted_iota(jnp.int32, (1536, 128), 1) < 2, 1.0, 0.0).astype(BF)

    wait(ag_y())
    start(ag_x(0))
    start(ag_x(1))
    for p in range(PAIRS):
        do_all[p] = nt(cot_ref[...], w_ref[p * 128 : p * 128 + 128, :]).astype(BF)
    wait(ag_x(0))
    start(ag_s(0))

    lo = lax.broadcasted_iota(jnp.int32, (QB, 128), 1) < 64
    lane2 = lax.broadcasted_iota(jnp.int32, (2 * QB, 128), 1)

    def compute(p):
        kx[0:512, :128] = halo[p, 0]
        kx[512:1024, :128] = k_ref[:, cols(p)]
        kx[1024:1536, :128] = mem[p, 0]
        vx[0:512, :128] = halo[p, 1]
        vx[512:1024, :128] = v_ref[:, cols(p)]
        vx[1024:1536, :128] = mem[p, 1]
        dkt[...] = jnp.zeros_like(dkt)
        dvt[...] = jnp.zeros_like(dvt)
        row2 = lax.broadcasted_iota(jnp.int32, (2 * QB, 128), 0)
        rr = lax.broadcasted_iota(jnp.int32, (2 * QB, QB), 0)
        rr = jnp.where(rr >= QB, rr - QB, rr)
        cc = lax.broadcasted_iota(jnp.int32, (2 * QB, QB), 1)
        zero = jnp.zeros((QB, 128), BF)
        memory = slice(1024, 1536)
        for b in range(512 // QB):
            rows = slice(b * QB, (b + 1) * QB)
            band = slice(b * QB, b * QB + BAND)
            qp = q_ref[rows, cols(p)] * jnp.asarray(0.125, BF)
            qs = jnp.concatenate([jnp.where(lo, qp, zero), jnp.where(lo, zero, qp)], 0)
            r2 = jnp.where(row2 >= QB, row2 - QB, row2) + b * QB
            onehot = jnp.where(lane2 == r2 // 128, 1.0, 0.0).astype(BF)
            qa = jnp.concatenate([qs, onehot], 1)
            sb = nt(qa, kx[band, :])
            sm = nt(qa, kx[memory, :])
            far = jnp.where(cc > rr, sb[:, :QB], NEG)
            near = jnp.where(cc <= rr, sb[:, 512:], NEG)
            s = jnp.concatenate([far, sb[:, QB:512], near, sm], 1)
            m = jnp.max(s, axis=1, keepdims=True)
            e = jnp.exp(s - m).astype(BF)
            eb, em = e[:, :BAND], e[:, BAND:]
            o = nn(eb, vx[band, :]) + nn(em, vx[memory, :])
            live = vcol[rows, 4:5]
            live = jnp.concatenate([live, live], 0)
            inv = live / jnp.maximum(o[:, 128:129], 1.0)
            a = o[:, :128] * inv
            dop = do_all[p, rows, :]
            dos = jnp.concatenate([jnp.where(lo, dop, zero), jnp.where(lo, zero, dop)], 0)
            dosf = dos.astype(F32)
            rd = jnp.sum(a * dosf, axis=1, keepdims=True)
            high = rd.astype(BF).astype(F32)
            tail = jnp.where(lane2 == 0, -high, jnp.where(lane2 == 1, high - rd, 0.0)).astype(BF)
            da = jnp.concatenate([dos, tail], 1)
            dsb = (eb.astype(F32) * nt(da, vx[band, :])).astype(BF)
            dsm = (em.astype(F32) * nt(da, vx[memory, :])).astype(BF)
            dqs = (nn(dsb, kx[band, :128]) + nn(dsm, kx[memory, :128])) * (inv * 0.125)
            dq_ref[rows, cols(p)] = jnp.where(lo, dqs[:QB], dqs[QB:]).astype(BF)
            att[rows, :] = jnp.where(lo, a[:QB], a[QB:]).astype(BF)
            qn = (qs.astype(F32) * inv).astype(BF)
            don = (dosf * inv).astype(BF)
            dkt[:, band] += tn(qn, dsb)
            dkt[:, memory] += tn(qn, dsm)
            dvt[:, band] += tn(don, eb)
            dvt[:, memory] += tn(don, em)
        for i, t in enumerate((dkt, dvt)):
            mg[p, i] = t[:, 1024:].T.astype(BF)
            bsend[p, i] = t[:, :512].T.astype(BF)
            own[p, i] = t[:, 512:1024].T
        for h in range(2):
            wb[p, h] = tn(att[...], cot_ref[:, h * 512 : h * 512 + 512]).astype(BF)

    def mem_sum_s(p):
        wait(mem_s(p))
        both = mg[p, :, part(core, 256), :].astype(F32) + srecv[p].astype(F32)
        xs[p] = both.astype(BF)
        start(mem_x(p))

    def mem_sum_x(p):
        wait(mem_x(p))
        total = xs[p, :, part(x, 64), :].astype(F32)
        for d in range(3):
            total += xrecv[p, d].astype(F32)
        ys[p] = total.astype(BF)
        start(mem_y(p))

    def mem_sum_y(p):
        wait(mem_y(p))
        wait(halo_back(p))
        total = ys[p, :, part(y, 16), :].astype(F32)
        for d in range(3):
            total += yrecv[p, d].astype(F32)
        high = total.astype(BF)
        low = (total - high.astype(F32)).astype(BF)
        for i, ref in enumerate((dk_ref, dv_ref)):
            grad = own[p, i] + brecv[p, i].astype(F32)
            grad += tn(pick_ref[...], high[i]) + tn(pick_ref[...], low[i])
            ref[:, cols(p)] = grad.astype(BF)

    def w_sum1(p):
        wait(wt1(p))
        ws2[p] = (wb[p, core].astype(F32) + w1[p].astype(F32)).astype(BF)
        start(wt2(p))

    def w_sum2(p):
        wait(wt2(p))
        total = ws2[p, part(z, 32), :].astype(F32)
        for d in range(3):
            total += w2[p, d].astype(F32)
        for c in range(4):
            ws3[p, c] = total[:, c * 128 : c * 128 + 128].astype(BF)
        start(wt3(p))

    def w_sum3(p):
        wait(wt3(p))
        total = ws3[p, y].astype(F32)
        for d in range(3):
            total += w3[p, d].astype(F32)
        ws4[p] = total
        start(wt4(p))

    def w_sum4(p):
        wait(wt4(p))
        total = ws4[p, part(x, 8), :]
        for d in range(3):
            total += w4[p, d]
        f5[p, part(x, 8), :] = total * (65536.0 ** -0.5)
        start(wt5(p))

    def w_put5(p):
        wait(wt5(p))
        f6[p, y] = f5[p].astype(BF)
        start(wt6(p))

    def w_put6(p):
        wait(wt6(p))
        for c in range(4):
            f7[p, part(z, 32), c * 128 : c * 128 + 128] = f6[p, c]
        start(wt7(p))

    def w_put7(p):
        wait(wt7(p))
        start(wt8(p))

    def w_put8(p):
        wait(wt8(p))
        rows = part(p, 128)
        wg_ref[rows, part(core, 512)] = f7[p].astype(F32)
        wg_ref[rows, part(1 - core, 512)] = f8[p].astype(F32)

    lagged = [
        (1, [mem_sum_s, w_sum1]),
        (2, [mem_sum_x, w_sum2]),
        (3, [mem_sum_y, w_sum3]),
        (4, [w_sum4]),
        (5, [w_put5]),
        (6, [w_put6]),
        (7, [w_put7]),
        (8, [w_put8]),
    ]

    def step(t, carry):
        @pl.when(t < PAIRS - 2)
        def _():
            start(ag_x(t + 2))
            start(halo_fwd(t + 2))

        @pl.when(t < PAIRS - 1)
        def _():
            wait(ag_x(t + 1))
            start(ag_s(t + 1))

        @pl.when(t < PAIRS)
        def _():
            wait(ag_s(t))
            wait(halo_fwd(t))
            compute(t)
            start(mem_s(t))
            start(wt1(t))
            start(halo_back(t))

        for lag, stages in lagged:

            @pl.when((t >= lag) & (t < PAIRS + lag))
            def _(lag=lag, stages=stages):
                for stage in stages:
                    stage(t - lag)

        return carry

    lax.fori_loop(0, PAIRS + 8, step, 0)


def per_device(queries, key_rows, value_rows, cotangent, out_weight, prot_blocks, last_fill, memory_slots):
    slots = memory_slots[0]
    own = lax.dynamic_slice_in_dim(slots, lax.axis_index("ctx") * 16, 16)
    pick = (own[:, None] == jnp.arange(512, dtype=jnp.int32)[None, :]).astype(BF)
    order = slots.reshape(16, 2, 16).transpose(1, 0, 2).reshape(1, 512)
    vmem = pl.BlockSpec(memory_space=pltpu.VMEM)
    smem = pl.BlockSpec(memory_space=pltpu.SMEM)
    dma = pltpu.SemaphoreType.DMA
    row = jax.ShapeDtypeStruct((512, 1024), BF)

    def buf(*shape, dtype=BF):
        return pltpu.VMEM(shape, dtype)

    sems = [(3,), (PAIRS, 3), (PAIRS,), (PAIRS, 2), (PAIRS,)]
    sems += [(PAIRS,), (PAIRS, 3), (PAIRS, 3)]
    sems += [(PAIRS,)] + [(PAIRS, 3)] * 6 + [(PAIRS,)]
    dq, dk, dv, weight = pl.pallas_call(
        kernel,
        out_shape=[row, row, row, jax.ShapeDtypeStruct((1024, 1024), F32)],
        in_specs=[vmem] * 7 + [smem] * 2,
        out_specs=[vmem] * 4,
        scratch_shapes=[
            buf(1536, 256), buf(1536, 256), buf(128, 1536, dtype=F32), buf(128, 1536, dtype=F32),
            buf(512, 128), buf(PAIRS, 512, 128), buf(512, 128, dtype=F32), buf(PAIRS, 2, 512, 128, dtype=F32),
            buf(PAIRS, 2, 512, 128), buf(PAIRS, 2, 512, 128), buf(PAIRS, 2, 512, 128), buf(PAIRS, 2, 512, 128),
            buf(PAIRS, 2, 512, 128), buf(PAIRS, 2, 256, 128), buf(PAIRS, 2, 256, 128), buf(PAIRS, 3, 2, 64, 128),
            buf(PAIRS, 2, 64, 128), buf(PAIRS, 3, 2, 16, 128),
            buf(PAIRS, 2, 128, 512), buf(PAIRS, 128, 512), buf(PAIRS, 128, 512), buf(PAIRS, 3, 32, 512),
            buf(PAIRS, 4, 32, 128), buf(PAIRS, 3, 32, 128), buf(PAIRS, 32, 128, dtype=F32),
            buf(PAIRS, 3, 8, 128, dtype=F32), buf(PAIRS, 32, 128, dtype=F32), buf(PAIRS, 4, 32, 128),
            buf(PAIRS, 128, 512), buf(PAIRS, 128, 512),
        ]
        + [dma(s) for s in sems for _ in range(2)],
        compiler_params=pltpu.CompilerParams(
            collective_id=0, has_side_effects=True, vmem_limit_bytes=62 * 2**20
        ),
        name="fused",
    )(
        queries[0], key_rows[0], value_rows[0], cotangent[0], out_weight, pick, order,
        prot_blocks, last_fill,
    )
    return dq[None], dk[None], dv[None], weight


def solution(mesh):
    row = P("fam", "ctx", None)
    fam = P("fam", None)
    return jax.shard_map(
        per_device,
        mesh=mesh,
        in_specs=(row, row, row, row, P(), fam, fam, fam),
        out_specs=(row, row, row, P()),
        check_vma=False,
    )
```

```python
import jax
import jax.numpy as jnp
from jax import lax
from jax.experimental import pallas as pl
from jax.experimental.pallas import tpu as pltpu
from jax.sharding import PartitionSpec as P

F32 = jnp.float32
BF = jnp.bfloat16
NEG = -1e30
QB = 256
BAND = 512 + QB
PAIRS = 8
LEAD = 2
RING = LEAD + 1
MESH = pl.DeviceIdType.MESH


def nt(a, b):
    return lax.dot_general(a, b, (((1,), (1,)), ((), ())), preferred_element_type=F32)


def nn(a, b):
    return lax.dot_general(a, b, (((1,), (0,)), ((), ())), preferred_element_type=F32)


def tn(a, b):
    return lax.dot_general(a, b, (((0,), (0,)), ((), ())), preferred_element_type=F32)


def cols(p):
    return pl.ds(pl.multiple_of(p * 128, 128), 128)


def part(index, size):
    return pl.ds(pl.multiple_of(index * size, size), size)


def kernel(
    q_ref, k_ref, v_ref, cot_ref, w_ref, slots_ref, slot_ref, blocks_ref, fill_ref,
    dq_ref, dk_ref, dv_ref, wg_ref,
    kv, ebuf, inv_buf, rd_buf, bias, pick_ref, dkt, dvt, att, do_all, vcol, own,
    bsend, brecv, mg, srecv, xs, xrecv, ys, yrecv,
    wb, w1, ws2, w2, ws3, w3, ws4, w4, f5, f6, f7,
    agy_s, agy_r, agx_s, agx_r, ags_s, ags_r, hal_s, hal_r, bak_s, bak_r,
    ms_s, ms_r, mx_s, mx_r, my_s, my_r,
    s1_s, s1_r, s2_s, s2_r, s3_s, s3_r, s4_s, s4_r, s5_s, s5_r, s6_s, s6_r, s7_s, s7_r, s8_s, s8_r,
):
    z = lax.axis_index("fam")
    me = lax.axis_index("ctx")
    x = me // 8
    y = (me // 2) % 4
    core = me % 2

    def at(xx, yy, cc):
        return (z, xx * 8 + yy * 2 + cc)

    sib = at(x, y, 1 - core)
    nxt = (z, (me + 1) % 32)
    prv = (z, (me + 31) % 32)
    across = (z, (me + 31 + 2 * core) % 32)
    ypeer = [at(x, (y + d) % 4, core) for d in (1, 2, 3)]
    xpeer = [at((x + d) % 4, y, core) for d in (1, 2, 3)]
    zpeer = [((z + d) % 4, me) for d in (1, 2, 3)]

    def rc(src, dst, send, recv, device):
        return pltpu.make_async_remote_copy(
            src_ref=src, dst_ref=dst, send_sem=send, recv_sem=recv, device_id=device, device_id_type=MESH
        )

    def ag_y():
        ref = kv.at[:, :, part(64 + core * 16 + x * 4 + y, 16)]
        return [rc(ref, ref, agy_s.at[d], agy_r.at[d], ypeer[d]) for d in range(3)]

    def ag_x(p):
        ref = kv.at[p, :, part(16 + core * 4 + x, 64)]
        return [rc(ref, ref, agx_s.at[p, d], agx_r.at[p, d], xpeer[d]) for d in range(3)]

    def ag_s(p):
        ref = kv.at[p, :, part(4 + core, 256)]
        return [rc(ref, ref, ags_s.at[p], ags_r.at[p], sib)]

    def halo_fwd(p):
        return [rc(kv.at[p, :, 512:1024], kv.at[p, :, 0:512], hal_s.at[p], hal_r.at[p], nxt)]

    def halo_back(p):
        return [rc(bsend.at[p], brecv.at[p], bak_s.at[p], bak_r.at[p], prv)]

    def mem_s(p):
        return [rc(mg.at[p, :, part(1 - core, 256)], srecv.at[p], ms_s.at[p], ms_r.at[p], sib)]

    def mem_x(p):
        return [
            rc(xs.at[p, :, part((x + d + 1) % 4, 64)], xrecv.at[p, d], mx_s.at[p, d], mx_r.at[p, d], xpeer[d])
            for d in range(3)
        ]

    def mem_y(p):
        return [
            rc(ys.at[p, :, part((y + d + 1) % 4, 16)], yrecv.at[p, d], my_s.at[p, d], my_r.at[p, d], ypeer[d])
            for d in range(3)
        ]

    def wt1(p):
        return [rc(wb.at[p, 1 - core], w1.at[p], s1_s.at[p], s1_r.at[p], sib)]

    def wt2(p):
        return [
            rc(ws2.at[p, part((z + d + 1) % 4, 32)], w2.at[p, d], s2_s.at[p, d], s2_r.at[p, d], zpeer[d])
            for d in range(3)
        ]

    def wt3(p):
        return [
            rc(ws3.at[p, (y + d + 1) % 4], w3.at[p, d], s3_s.at[p, d], s3_r.at[p, d], ypeer[d])
            for d in range(3)
        ]

    def wt4(p):
        return [
            rc(ws4.at[p, part((x + d + 1) % 4, 8)], w4.at[p, d], s4_s.at[p, d], s4_r.at[p, d], xpeer[d])
            for d in range(3)
        ]

    def wt5(p):
        ref = f5.at[p, part(x, 8)]
        return [rc(ref, ref, s5_s.at[p, d], s5_r.at[p, d], xpeer[d]) for d in range(3)]

    def wt6(p):
        ref = f6.at[p, y]
        return [rc(ref, ref, s6_s.at[p, d], s6_r.at[p, d], ypeer[d]) for d in range(3)]

    def wt7(p):
        ref = f7.at[p, core, part(z, 32)]
        return [rc(ref, ref, s7_s.at[p, d], s7_r.at[p, d], zpeer[d]) for d in range(3)]

    def wt8(p):
        return [rc(f7.at[p, core], f7.at[p, core], s8_s.at[p], s8_r.at[p], sib)]

    def start(copies):
        for c in copies:
            c.start()

    def wait(copies):
        for c in copies:
            c.wait()

    barrier = pltpu.get_barrier_semaphore()
    for device in [sib, across] + ypeer + xpeer + zpeer:
        pl.semaphore_signal(barrier, inc=1, device_id=device, device_id_type=MESH)
    wide = lax.broadcasted_iota(jnp.int32, (16, 512), 1)
    line = lax.broadcasted_iota(jnp.int32, (16, 512), 0)
    chosen = jnp.zeros((16, 512), jnp.int32)
    for i in range(16):
        chosen = jnp.where(line == i, slot_ref[0, me * 16 + i], chosen)
    pick = jnp.where(wide == chosen, 1.0, 0.0).astype(BF)
    pick_ref[...] = pick
    mine = part(64 + core * 16 + x * 4 + y, 16)
    for i, r in enumerate((k_ref, v_ref)):
        for p in range(PAIRS):
            kv[p, i, 512:1024, :] = r[:, p * 128 : p * 128 + 128]
            kv[p, i, mine, :] = nn(pick, r[:, p * 128 : p * 128 + 128]).astype(BF)
    pl.semaphore_wait(barrier, 11)
    start(ag_y())
    start(halo_fwd(0))
    start(halo_fwd(1))

    here = lax.broadcasted_iota(jnp.int32, (512, 512), 1)
    there = lax.broadcasted_iota(jnp.int32, (512, 512), 0)
    origin = ((here // 16) % 16) * 32 + (here // 256) * 16 + here % 16
    move = jnp.where(there == origin, 1.0, 0.0).astype(BF)
    slots = jnp.broadcast_to(slots_ref[...], (16, 512))
    halves = nn((slots // 2).astype(F32).astype(BF), move)
    odds = nn((slots % 2).astype(F32).astype(BF), move)
    slots = (halves * 2.0 + odds).astype(jnp.int32)[:1]

    pos_band = me * 512 - 512 + lax.broadcasted_iota(jnp.int32, (1, 1024), 1)
    order = lax.broadcasted_iota(jnp.int32, (1, 512), 1) // 16
    holder = (order % 16) * 2 + order // 16
    pos = jnp.concatenate([pos_band, holder * 512 + slots], axis=1)
    block = (pos + 512) // 128 - 4
    prot = jnp.zeros((1, 1536), jnp.int32)
    limit = jnp.zeros((1, 1536), jnp.int32)
    first = jnp.int32(0)
    for i in range(32):
        end = first + blocks_ref[0, i]
        inside = (block >= first) & (block < end)
        prot = jnp.where(inside, i, prot)
        limit = jnp.where(inside, (end - 1) * 128 + fill_ref[0, i], limit)
        first = end
    real = (pos >= 0) & (pos < limit)
    is_mem = lax.broadcasted_iota(jnp.int32, (1, 1536), 1) >= 1024
    rows8 = lax.broadcasted_iota(jnp.int32, (8, 1536), 0)
    table = jnp.where(rows8 == 4, jnp.where(real, 1.0, 0.0), 0.0)
    for a in range(4):
        mine_prot = prot[:, 512 + a * 128 : 513 + a * 128]
        seen = real & ((is_mem & (prot < mine_prot)) | (jnp.logical_not(is_mem) & (prot == mine_prot)))
        table = jnp.where(rows8 == a, jnp.where(seen, 0.0, NEG), table)
    bias[...] = table
    vcol[...] = jnp.concatenate([table[:, 512:1024], jnp.zeros((120, 512), F32)], axis=0).T

    wait(ag_y())
    start(ag_x(0))
    start(ag_x(1))
    wait(ag_x(0))
    start(ag_s(0))

    lo = lax.broadcasted_iota(jnp.int32, (QB, 128), 1) < 64
    zero = jnp.zeros((QB, 128), BF)
    memory = slice(1024, 1536)

    def stacked(pair):
        return jnp.concatenate([jnp.where(lo, pair, zero), jnp.where(lo, zero, pair)], 0)

    def forward(p):
        slot = p % RING
        do_all[p] = nt(cot_ref[...], w_ref[part(p, 128), :]).astype(BF)
        rr = lax.broadcasted_iota(jnp.int32, (128, QB), 0)
        cc = lax.broadcasted_iota(jnp.int32, (128, QB), 1)
        for b in range(512 // QB):
            rows = slice(b * QB, (b + 1) * QB)
            band = slice(b * QB, b * QB + BAND)
            qs = stacked(q_ref[rows, cols(p)] * jnp.asarray(0.125, BF))
            sb = nt(qs, kv[p, 0, band, :])
            sm = nt(qs, kv[p, 0, memory, :])
            sums = []
            exps = []
            for g in range(2 * QB // 128):
                sub = g % (QB // 128)
                a = b * QB // 128 + sub
                group = slice(g * 128, g * 128 + 128)
                s = sb[group] + bias[a : a + 1, band]
                far = jnp.where(cc > rr + sub * 128, s[:, :QB], NEG)
                near = jnp.where(cc <= rr + sub * 128, s[:, 512:], NEG)
                s = jnp.concatenate([far, s[:, QB:512], near, sm[group] + bias[a : a + 1, memory]], 1)
                e = jnp.exp(s - jnp.max(s, axis=1, keepdims=True))
                sums.append(jnp.sum(e, axis=1, keepdims=True))
                exps.append(e.astype(BF))
            e = jnp.concatenate(exps, 0)
            ebuf[slot, b] = e
            o = nn(e[:, :BAND], kv[p, 1, band, :]) + nn(e[:, BAND:], kv[p, 1, memory, :])
            live = vcol[rows, 4:5]
            inv = jnp.concatenate([live, live], 0) / jnp.maximum(jnp.concatenate(sums, 0), 1.0)
            a = o * inv
            inv_buf[slot, b] = inv
            rd_buf[slot, b] = jnp.sum(a * stacked(do_all[p, rows, :]).astype(F32), axis=1, keepdims=True)
            att[rows, :] = jnp.where(lo, a[:QB], a[QB:]).astype(BF)
        for h in range(2):
            wb[p, h] = tn(att[...], cot_ref[:, h * 512 : h * 512 + 512]).astype(BF)

    def backward(p):
        slot = p % RING
        dkt[...] = jnp.zeros_like(dkt)
        dvt[...] = jnp.zeros_like(dvt)
        for b in range(512 // QB):
            rows = slice(b * QB, (b + 1) * QB)
            band = slice(b * QB, b * QB + BAND)
            inv = inv_buf[slot, b]
            rd = rd_buf[slot, b]
            dos = stacked(do_all[p, rows, :])
            eb = ebuf[slot, b, :, :BAND]
            em = ebuf[slot, b, :, BAND:]
            dsb = (eb.astype(F32) * (nt(dos, kv[p, 1, band, :]) - rd)).astype(BF)
            dsm = (em.astype(F32) * (nt(dos, kv[p, 1, memory, :]) - rd)).astype(BF)
            dqs = (nn(dsb, kv[p, 0, band, :]) + nn(dsm, kv[p, 0, memory, :])) * (inv * 0.125)
            dq_ref[rows, cols(p)] = jnp.where(lo, dqs[:QB], dqs[QB:]).astype(BF)
            qs = stacked(q_ref[rows, cols(p)] * jnp.asarray(0.125, BF))
            qn = (qs.astype(F32) * inv).astype(BF)
            don = (dos.astype(F32) * inv).astype(BF)
            dkt[:, band] += tn(qn, dsb)
            dkt[:, memory] += tn(qn, dsm)
            dvt[:, band] += tn(don, eb)
            dvt[:, memory] += tn(don, em)
        for i, t in enumerate((dkt, dvt)):
            mg[p, i] = t[:, 1024:].T.astype(BF)
            bsend[p, i] = t[:, :512].T.astype(BF)
            own[p, i] = t[:, 512:1024].T

    def mem_sum_s(p):
        wait(mem_s(p))
        both = mg[p, :, part(core, 256), :].astype(F32) + srecv[p].astype(F32)
        xs[p] = both.astype(BF)
        start(mem_x(p))

    def mem_sum_x(p):
        wait(mem_x(p))
        total = xs[p, :, part(x, 64), :].astype(F32)
        for d in range(3):
            total += xrecv[p, d].astype(F32)
        ys[p] = total.astype(BF)
        start(mem_y(p))

    def mem_sum_y(p):
        wait(mem_y(p))
        wait(halo_back(p))
        total = ys[p, :, part(y, 16), :].astype(F32)
        for d in range(3):
            total += yrecv[p, d].astype(F32)
        high = total.astype(BF)
        low = (total - high.astype(F32)).astype(BF)
        for i, ref in enumerate((dk_ref, dv_ref)):
            grad = own[p, i] + brecv[p, i].astype(F32)
            grad += tn(pick_ref[...], high[i]) + tn(pick_ref[...], low[i])
            ref[:, cols(p)] = grad.astype(BF)

    def w_sum1(p):
        wait(wt1(p))
        ws2[p] = (wb[p, core].astype(F32) + w1[p].astype(F32)).astype(BF)
        start(wt2(p))

    def w_sum2(p):
        wait(wt2(p))
        total = ws2[p, part(z, 32), :].astype(F32)
        for d in range(3):
            total += w2[p, d].astype(F32)
        for c in range(4):
            ws3[p, c] = total[:, c * 128 : c * 128 + 128].astype(BF)
        start(wt3(p))

    def w_sum3(p):
        wait(wt3(p))
        total = ws3[p, y].astype(F32)
        for d in range(3):
            total += w3[p, d].astype(F32)
        ws4[p] = total
        start(wt4(p))

    def w_sum4(p):
        wait(wt4(p))
        total = ws4[p, part(x, 8), :]
        for d in range(3):
            total += w4[p, d]
        f5[p, part(x, 8), :] = total * (65536.0 ** -0.5)
        start(wt5(p))

    def w_put5(p):
        wait(wt5(p))
        f6[p, y] = f5[p].astype(BF)
        start(wt6(p))

    def w_put6(p):
        wait(wt6(p))
        for c in range(4):
            f7[p, core, part(z, 32), c * 128 : c * 128 + 128] = f6[p, c]
        start(wt7(p))

    def w_put7(p):
        wait(wt7(p))
        start(wt8(p))

    def w_put8(p):
        wait(wt8(p))
        rows = part(p, 128)
        for h in range(2):
            wg_ref[rows, h * 512 : h * 512 + 512] = f7[p, h].astype(F32)

    between = [
        (1, w_sum2), (LEAD + 1, mem_sum_s), (2, w_sum4), (3, w_put6), (4, w_put8), (LEAD + 2, mem_sum_y),
    ]
    after = [(0, w_sum1), (1, w_sum3), (LEAD + 1, mem_sum_x), (2, w_put5), (3, w_put7)]

    def run(t, stages):
        for lag, stage in stages:

            @pl.when((t >= lag) & (t < PAIRS + lag))
            def _(lag=lag, stage=stage):
                stage(t - lag)

    def step(t, carry):
        @pl.when(t < PAIRS - 2)
        def _():
            start(ag_x(t + 2))
            start(halo_fwd(t + 2))

        @pl.when(t < PAIRS - 1)
        def _():
            wait(ag_x(t + 1))
            start(ag_s(t + 1))

        @pl.when(t < PAIRS)
        def _():
            wait(ag_s(t))
            wait(halo_fwd(t))
            forward(t)
            start(wt1(t))

        run(t, between)

        @pl.when((t >= LEAD) & (t < PAIRS + LEAD))
        def _():
            backward(t - LEAD)
            start(mem_s(t - LEAD))
            start(halo_back(t - LEAD))

        run(t, after)
        return carry

    lax.fori_loop(0, PAIRS + LEAD + 2, step, 0)


def handed_on(*refs):
    sources, targets, sems = refs[:4], refs[4:8], refs[8]
    copies = [pltpu.make_async_copy(a, b, sems.at[i]) for i, (a, b) in enumerate(zip(sources, targets))]
    for c in copies:
        c.start()
    for c in copies:
        c.wait()


def per_device(queries, key_rows, value_rows, cotangent, out_weight, prot_blocks, last_fill, memory_slots):
    vmem = pl.BlockSpec(memory_space=pltpu.VMEM)
    smem = pl.BlockSpec(memory_space=pltpu.SMEM)
    dma = pltpu.SemaphoreType.DMA
    row = jax.ShapeDtypeStruct((512, 1024), BF)

    def buf(*shape, dtype=BF):
        return pltpu.VMEM(shape, dtype)

    sems = [(3,), (PAIRS, 3), (PAIRS,), (PAIRS,), (PAIRS,)]
    sems += [(PAIRS,), (PAIRS, 3), (PAIRS, 3)]
    sems += [(PAIRS,)] + [(PAIRS, 3)] * 6 + [(PAIRS,)]
    shapes = [row, row, row, jax.ShapeDtypeStruct((1024, 1024), F32)]
    outs = pl.pallas_call(
        kernel,
        out_shape=shapes,
        in_specs=[vmem] * 6 + [smem] * 3,
        out_specs=[vmem] * 4,
        scratch_shapes=[
            buf(PAIRS, 2, 1536, 128), buf(RING, 512 // QB, 2 * QB, BAND + 512),
            buf(RING, 512 // QB, 2 * QB, 1, dtype=F32), buf(RING, 512 // QB, 2 * QB, 1, dtype=F32),
            buf(8, 1536, dtype=F32), buf(16, 512), buf(128, 1536, dtype=F32), buf(128, 1536, dtype=F32),
            buf(512, 128), buf(PAIRS, 512, 128), buf(512, 128, dtype=F32), buf(PAIRS, 2, 512, 128, dtype=F32),
            buf(PAIRS, 2, 512, 128), buf(PAIRS, 2, 512, 128),
            buf(PAIRS, 2, 512, 128), buf(PAIRS, 2, 256, 128), buf(PAIRS, 2, 256, 128), buf(PAIRS, 3, 2, 64, 128),
            buf(PAIRS, 2, 64, 128), buf(PAIRS, 3, 2, 16, 128),
            buf(PAIRS, 2, 128, 512), buf(PAIRS, 128, 512), buf(PAIRS, 128, 512), buf(PAIRS, 3, 32, 512),
            buf(PAIRS, 4, 32, 128), buf(PAIRS, 3, 32, 128), buf(PAIRS, 32, 128, dtype=F32),
            buf(PAIRS, 3, 8, 128, dtype=F32), buf(PAIRS, 32, 128, dtype=F32), buf(PAIRS, 4, 32, 128),
            buf(PAIRS, 2, 128, 512),
        ]
        + [dma(s) for s in sems for _ in range(2)],
        compiler_params=pltpu.CompilerParams(
            collective_id=0, has_side_effects=True, vmem_limit_bytes=62 * 2**20
        ),
        name="fused",
    )(
        queries[0], key_rows[0], value_rows[0], cotangent[0], out_weight, memory_slots,
        memory_slots, prot_blocks, last_fill,
    )
    hbm = pl.BlockSpec(memory_space=pl.ANY)
    dq, dk, dv, weight = pl.pallas_call(
        handed_on,
        out_shape=shapes,
        in_specs=[hbm] * 4,
        out_specs=[hbm] * 4,
        scratch_shapes=[dma((4,))],
        name="handed_on",
    )(*outs)
    return dq[None], dk[None], dv[None], weight


def solution(mesh):
    row = P("fam", "ctx", None)
    fam = P("fam", None)
    return jax.shard_map(
        per_device,
        mesh=mesh,
        in_specs=(row, row, row, row, P(), fam, fam, fam),
        out_specs=(row, row, row, P()),
        check_vma=False,
    )
```

```python
import jax
import jax.numpy as jnp
from jax import lax
from jax.experimental import pallas as pl
from jax.experimental.pallas import tpu as pltpu
from jax.sharding import PartitionSpec as P

F32 = jnp.float32
BF = jnp.bfloat16
NEG = -1e30
QB = 256
BAND = 512 + QB
PAIRS = 8
LEAD = 2
RING = LEAD + 1
MESH = pl.DeviceIdType.MESH


def nt(a, b):
    return lax.dot_general(a, b, (((1,), (1,)), ((), ())), preferred_element_type=F32)


def nn(a, b):
    return lax.dot_general(a, b, (((1,), (0,)), ((), ())), preferred_element_type=F32)


def tn(a, b):
    return lax.dot_general(a, b, (((0,), (0,)), ((), ())), preferred_element_type=F32)


def cols(p):
    return pl.ds(pl.multiple_of(p * 128, 128), 128)


def part(index, size):
    return pl.ds(pl.multiple_of(index * size, size), size)


def kernel(
    q_ref, k_ref, v_ref, cot_ref, w_ref, slots_ref, slot_ref, blocks_ref, fill_ref,
    dq_ref, dk_ref, dv_ref, wg_ref,
    kv, ebuf, inv_buf, rd_buf, bias, pick_ref, dkt, dvt, att, do_all, vcol, own,
    bsend, brecv, mg, srecv, xs, xrecv, ys, yrecv,
    wb, w1, ws2, w2, ws3, w3, ws4, w4, f5, f6, f7,
    agy_s, agy_r, agx_s, agx_r, ags_s, ags_r, hal_s, hal_r, bak_s, bak_r,
    ms_s, ms_r, mx_s, mx_r, my_s, my_r,
    s1_s, s1_r, s2_s, s2_r, s3_s, s3_r, s4_s, s4_r, s5_s, s5_r, s6_s, s6_r, s7_s, s7_r, s8_s, s8_r,
):
    z = lax.axis_index("fam")
    me = lax.axis_index("ctx")
    x = me // 8
    y = (me // 2) % 4
    core = me % 2

    def at(xx, yy, cc):
        return (z, xx * 8 + yy * 2 + cc)

    sib = at(x, y, 1 - core)
    nxt = (z, (me + 1) % 32)
    prv = (z, (me + 31) % 32)
    across = (z, (me + 31 + 2 * core) % 32)
    ypeer = [at(x, (y + d) % 4, core) for d in (1, 2, 3)]
    xpeer = [at((x + d) % 4, y, core) for d in (1, 2, 3)]
    zpeer = [((z + d) % 4, me) for d in (1, 2, 3)]

    def rc(src, dst, send, recv, device):
        return pltpu.make_async_remote_copy(
            src_ref=src, dst_ref=dst, send_sem=send, recv_sem=recv, device_id=device, device_id_type=MESH
        )

    def ag_y():
        ref = kv.at[:, :, part(64 + core * 16 + x * 4 + y, 16)]
        return [rc(ref, ref, agy_s.at[d], agy_r.at[d], ypeer[d]) for d in range(3)]

    def ag_x(p):
        ref = kv.at[p, :, part(16 + core * 4 + x, 64)]
        return [rc(ref, ref, agx_s.at[p, d], agx_r.at[p, d], xpeer[d]) for d in range(3)]

    def ag_s(p):
        ref = kv.at[p, :, part(4 + core, 256)]
        return [rc(ref, ref, ags_s.at[p], ags_r.at[p], sib)]

    def halo_fwd(p):
        return [rc(kv.at[p, :, 512:1024], kv.at[p, :, 0:512], hal_s.at[p], hal_r.at[p], nxt)]

    def halo_back(p):
        return [rc(bsend.at[p], brecv.at[p], bak_s.at[p], bak_r.at[p], prv)]

    def mem_s(p):
        return [rc(mg.at[p, :, part(1 - core, 256)], srecv.at[p], ms_s.at[p], ms_r.at[p], sib)]

    def mem_x(p):
        return [
            rc(xs.at[p, :, part((x + 3 - d) % 4, 64)], xrecv.at[p, d], mx_s.at[p, d], mx_r.at[p, d], xpeer[2 - d])
            for d in range(3)
        ]

    def mem_y(p):
        return [
            rc(ys.at[p, :, part((y + d + 1) % 4, 16)], yrecv.at[p, d], my_s.at[p, d], my_r.at[p, d], ypeer[d])
            for d in range(3)
        ]

    def wt1(p):
        return [rc(wb.at[p, 1 - core], w1.at[p], s1_s.at[p], s1_r.at[p], sib)]

    def wt2(p):
        return [
            rc(ws2.at[p, part((z + d + 1) % 4, 32)], w2.at[p, d], s2_s.at[p, d], s2_r.at[p, d], zpeer[d])
            for d in range(3)
        ]

    def wt3(p):
        return [
            rc(ws3.at[p, (y + d + 1) % 4], w3.at[p, d], s3_s.at[p, d], s3_r.at[p, d], ypeer[d])
            for d in range(3)
        ]

    def wt4(p):
        return [
            rc(ws4.at[p, part((x + d + 1) % 4, 8)], w4.at[p, d], s4_s.at[p, d], s4_r.at[p, d], xpeer[d])
            for d in range(3)
        ]

    def wt5(p):
        ref = f5.at[p, part(x, 8)]
        return [rc(ref, ref, s5_s.at[p, d], s5_r.at[p, d], xpeer[d]) for d in range(3)]

    def wt6(p):
        ref = f6.at[p, y]
        return [rc(ref, ref, s6_s.at[p, d], s6_r.at[p, d], ypeer[d]) for d in range(3)]

    def wt7(p):
        ref = f7.at[p, core, part(z, 32)]
        return [rc(ref, ref, s7_s.at[p, d], s7_r.at[p, d], zpeer[d]) for d in range(3)]

    def wt8(p):
        return [rc(f7.at[p, core], f7.at[p, core], s8_s.at[p], s8_r.at[p], sib)]

    def start(copies):
        for c in copies:
            c.start()

    def wait(copies):
        for c in copies:
            c.wait()

    def start_up(copies):
        for d, c in enumerate(copies):
            pl.when(x + d + 1 < 4)(c.start)

    def wait_up(copies):
        for d, c in enumerate(copies):
            pl.when(x + d + 1 < 4)(c.wait_send)
            pl.when(x >= d + 1)(c.wait_recv)

    def start_down(copies):
        for d, c in enumerate(copies):
            pl.when(x >= d + 1)(c.start)

    def wait_down(copies):
        for d, c in enumerate(copies):
            pl.when(x >= d + 1)(c.wait_send)
            pl.when(x + d + 1 < 4)(c.wait_recv)

    def start_fwd(p):
        pl.when(me < 31)(halo_fwd(p)[0].start)

    def wait_fwd(p):
        pl.when(me < 31)(halo_fwd(p)[0].wait_send)
        pl.when(me > 0)(halo_fwd(p)[0].wait_recv)

    def start_back(p):
        pl.when(me > 0)(halo_back(p)[0].start)

    def wait_back(p):
        pl.when(me > 0)(halo_back(p)[0].wait_send)
        pl.when(me < 31)(halo_back(p)[0].wait_recv)

    for p in range(PAIRS):
        kv[p, :, 0:512, :] = jnp.zeros((2, 512, 128), BF)
        kv[p, :, 1024:1536, :] = jnp.zeros((2, 512, 128), BF)
        xrecv[p] = jnp.zeros((3, 2, 64, 128), BF)

    @pl.when(me == 31)
    def _():
        for p in range(PAIRS):
            brecv[p] = jnp.zeros((2, 512, 128), BF)

    barrier = pltpu.get_barrier_semaphore()
    for device in [sib, across] + ypeer + xpeer + zpeer:
        pl.semaphore_signal(barrier, inc=1, device_id=device, device_id_type=MESH)
    wide = lax.broadcasted_iota(jnp.int32, (16, 512), 1)
    line = lax.broadcasted_iota(jnp.int32, (16, 512), 0)
    chosen = jnp.zeros((16, 512), jnp.int32)
    for i in range(16):
        chosen = jnp.where(line == i, slot_ref[0, me * 16 + i], chosen)
    pick = jnp.where(wide == chosen, 1.0, 0.0).astype(BF)
    pick_ref[...] = pick
    mine = part(64 + core * 16 + x * 4 + y, 16)
    for i, r in enumerate((k_ref, v_ref)):
        for p in range(PAIRS):
            kv[p, i, 512:1024, :] = r[:, p * 128 : p * 128 + 128]
            kv[p, i, mine, :] = nn(pick, r[:, p * 128 : p * 128 + 128]).astype(BF)
    pl.semaphore_wait(barrier, 11)
    start(ag_y())
    start_fwd(0)
    start_fwd(1)

    here = lax.broadcasted_iota(jnp.int32, (512, 512), 1)
    there = lax.broadcasted_iota(jnp.int32, (512, 512), 0)
    origin = ((here // 16) % 16) * 32 + (here // 256) * 16 + here % 16
    move = jnp.where(there == origin, 1.0, 0.0).astype(BF)
    slots = jnp.broadcast_to(slots_ref[...], (16, 512))
    halves = nn((slots // 2).astype(F32).astype(BF), move)
    odds = nn((slots % 2).astype(F32).astype(BF), move)
    slots = (halves * 2.0 + odds).astype(jnp.int32)[:1]

    pos_band = me * 512 - 512 + lax.broadcasted_iota(jnp.int32, (1, 1024), 1)
    order = lax.broadcasted_iota(jnp.int32, (1, 512), 1) // 16
    holder = (order % 16) * 2 + order // 16
    pos = jnp.concatenate([pos_band, holder * 512 + slots], axis=1)
    block = (pos + 512) // 128 - 4
    prot = jnp.zeros((1, 1536), jnp.int32)
    limit = jnp.zeros((1, 1536), jnp.int32)
    first = jnp.int32(0)
    for i in range(32):
        end = first + blocks_ref[0, i]
        inside = (block >= first) & (block < end)
        prot = jnp.where(inside, i, prot)
        limit = jnp.where(inside, (end - 1) * 128 + fill_ref[0, i], limit)
        first = end
    real = (pos >= 0) & (pos < limit)
    is_mem = lax.broadcasted_iota(jnp.int32, (1, 1536), 1) >= 1024
    rows8 = lax.broadcasted_iota(jnp.int32, (8, 1536), 0)
    table = jnp.where(rows8 == 4, jnp.where(real, 1.0, 0.0), 0.0)
    for a in range(4):
        mine_prot = prot[:, 512 + a * 128 : 513 + a * 128]
        seen = real & ((is_mem & (prot < mine_prot)) | (jnp.logical_not(is_mem) & (prot == mine_prot)))
        table = jnp.where(rows8 == a, jnp.where(seen, 0.0, NEG), table)
    bias[...] = table
    vcol[...] = jnp.concatenate([table[:, 512:1024], jnp.zeros((120, 512), F32)], axis=0).T

    wait(ag_y())
    start_up(ag_x(0))
    start_up(ag_x(1))
    wait_up(ag_x(0))
    start(ag_s(0))

    lo = lax.broadcasted_iota(jnp.int32, (QB, 128), 1) < 64
    zero = jnp.zeros((QB, 128), BF)
    memory = slice(1024, 1536)

    def stacked(pair):
        return jnp.concatenate([jnp.where(lo, pair, zero), jnp.where(lo, zero, pair)], 0)

    def forward(p):
        slot = p % RING
        do_all[p] = nt(cot_ref[...], w_ref[part(p, 128), :]).astype(BF)
        rr = lax.broadcasted_iota(jnp.int32, (128, QB), 0)
        cc = lax.broadcasted_iota(jnp.int32, (128, QB), 1)
        for b in range(512 // QB):
            rows = slice(b * QB, (b + 1) * QB)
            band = slice(b * QB, b * QB + BAND)
            qs = stacked(q_ref[rows, cols(p)] * jnp.asarray(0.125, BF))
            sb = nt(qs, kv[p, 0, band, :])
            sm = nt(qs, kv[p, 0, memory, :])
            sums = []
            exps = []
            for g in range(2 * QB // 128):
                sub = g % (QB // 128)
                a = b * QB // 128 + sub
                group = slice(g * 128, g * 128 + 128)
                s = sb[group] + bias[a : a + 1, band]
                far = jnp.where(cc > rr + sub * 128, s[:, :QB], NEG)
                near = jnp.where(cc <= rr + sub * 128, s[:, 512:], NEG)
                s = jnp.concatenate([far, s[:, QB:512], near, sm[group] + bias[a : a + 1, memory]], 1)
                e = jnp.exp(s - jnp.max(s, axis=1, keepdims=True))
                sums.append(jnp.sum(e, axis=1, keepdims=True))
                exps.append(e.astype(BF))
            e = jnp.concatenate(exps, 0)
            ebuf[slot, b] = e
            o = nn(e[:, :BAND], kv[p, 1, band, :]) + nn(e[:, BAND:], kv[p, 1, memory, :])
            live = vcol[rows, 4:5]
            inv = jnp.concatenate([live, live], 0) / jnp.maximum(jnp.concatenate(sums, 0), 1.0)
            a = o * inv
            inv_buf[slot, b] = inv
            rd_buf[slot, b] = jnp.sum(a * stacked(do_all[p, rows, :]).astype(F32), axis=1, keepdims=True)
            att[rows, :] = jnp.where(lo, a[:QB], a[QB:]).astype(BF)
        for h in range(2):
            wb[p, h] = tn(att[...], cot_ref[:, h * 512 : h * 512 + 512]).astype(BF)

    def backward(p):
        slot = p % RING
        dkt[...] = jnp.zeros_like(dkt)
        dvt[...] = jnp.zeros_like(dvt)
        for b in range(512 // QB):
            rows = slice(b * QB, (b + 1) * QB)
            band = slice(b * QB, b * QB + BAND)
            inv = inv_buf[slot, b]
            rd = rd_buf[slot, b]
            dos = stacked(do_all[p, rows, :])
            eb = ebuf[slot, b, :, :BAND]
            em = ebuf[slot, b, :, BAND:]
            dsb = (eb.astype(F32) * (nt(dos, kv[p, 1, band, :]) - rd)).astype(BF)
            dsm = (em.astype(F32) * (nt(dos, kv[p, 1, memory, :]) - rd)).astype(BF)
            dqs = (nn(dsb, kv[p, 0, band, :]) + nn(dsm, kv[p, 0, memory, :])) * (inv * 0.125)
            dq_ref[rows, cols(p)] = jnp.where(lo, dqs[:QB], dqs[QB:]).astype(BF)
            qs = stacked(q_ref[rows, cols(p)] * jnp.asarray(0.125, BF))
            qn = (qs.astype(F32) * inv).astype(BF)
            don = (dos.astype(F32) * inv).astype(BF)
            dkt[:, band] += tn(qn, dsb)
            dkt[:, memory] += tn(qn, dsm)
            dvt[:, band] += tn(don, eb)
            dvt[:, memory] += tn(don, em)
        for i, t in enumerate((dkt, dvt)):
            mg[p, i] = t[:, 1024:].T.astype(BF)
            bsend[p, i] = t[:, :512].T.astype(BF)
            own[p, i] = t[:, 512:1024].T

    def mem_sum_s(p):
        wait(mem_s(p))
        both = mg[p, :, part(core, 256), :].astype(F32) + srecv[p].astype(F32)
        xs[p] = both.astype(BF)
        start_down(mem_x(p))

    def mem_sum_x(p):
        wait_down(mem_x(p))
        total = xs[p, :, part(x, 64), :].astype(F32)
        for d in range(3):
            total += xrecv[p, d].astype(F32)
        ys[p] = total.astype(BF)
        start(mem_y(p))

    def mem_sum_y(p):
        wait(mem_y(p))
        wait_back(p)
        total = ys[p, :, part(y, 16), :].astype(F32)
        for d in range(3):
            total += yrecv[p, d].astype(F32)
        high = total.astype(BF)
        low = (total - high.astype(F32)).astype(BF)
        for i, ref in enumerate((dk_ref, dv_ref)):
            grad = own[p, i] + brecv[p, i].astype(F32)
            grad += tn(pick_ref[...], high[i]) + tn(pick_ref[...], low[i])
            ref[:, cols(p)] = grad.astype(BF)

    def w_sum1(p):
        wait(wt1(p))
        ws2[p] = (wb[p, core].astype(F32) + w1[p].astype(F32)).astype(BF)
        start(wt2(p))

    def w_sum2(p):
        wait(wt2(p))
        total = ws2[p, part(z, 32), :].astype(F32)
        for d in range(3):
            total += w2[p, d].astype(F32)
        for c in range(4):
            ws3[p, c] = total[:, c * 128 : c * 128 + 128].astype(BF)
        start(wt3(p))

    def w_sum3(p):
        wait(wt3(p))
        total = ws3[p, y].astype(F32)
        for d in range(3):
            total += w3[p, d].astype(F32)
        ws4[p] = total
        start(wt4(p))

    def w_sum4(p):
        wait(wt4(p))
        total = ws4[p, part(x, 8), :]
        for d in range(3):
            total += w4[p, d]
        f5[p, part(x, 8), :] = total * (65536.0 ** -0.5)
        start(wt5(p))

    def w_put5(p):
        wait(wt5(p))
        f6[p, y] = f5[p].astype(BF)
        start(wt6(p))

    def w_put6(p):
        wait(wt6(p))
        for c in range(4):
            f7[p, core, part(z, 32), c * 128 : c * 128 + 128] = f6[p, c]
        start(wt7(p))

    def w_put7(p):
        wait(wt7(p))
        start(wt8(p))

    def w_put8(p):
        wait(wt8(p))
        rows = part(p, 128)
        for h in range(2):
            wg_ref[rows, h * 512 : h * 512 + 512] = f7[p, h]

    between = [
        (1, w_sum2), (LEAD + 1, mem_sum_s), (2, w_sum4), (3, w_put6), (4, w_put8), (LEAD + 2, mem_sum_y),
    ]
    after = [(0, w_sum1), (1, w_sum3), (LEAD + 1, mem_sum_x), (2, w_put5), (3, w_put7)]

    def run(t, stages):
        for lag, stage in stages:

            @pl.when((t >= lag) & (t < PAIRS + lag))
            def _(lag=lag, stage=stage):
                stage(t - lag)

    def step(t, carry):
        @pl.when(t < PAIRS - 2)
        def _():
            start_up(ag_x(t + 2))
            start_fwd(t + 2)

        @pl.when(t < PAIRS - 1)
        def _():
            wait_up(ag_x(t + 1))
            start(ag_s(t + 1))

        @pl.when(t < PAIRS)
        def _():
            wait(ag_s(t))
            wait_fwd(t)
            forward(t)
            start(wt1(t))

        run(t, between)

        @pl.when((t >= LEAD) & (t < PAIRS + LEAD))
        def _():
            backward(t - LEAD)
            start(mem_s(t - LEAD))
            start_back(t - LEAD)

        run(t, after)
        return carry

    lax.fori_loop(0, PAIRS + LEAD + 2, step, 0)


def handed_on(*refs):
    for source, target in zip(refs[:4], refs[4:]):
        target[...] = source[...].astype(target.dtype)


def per_device(queries, key_rows, value_rows, cotangent, out_weight, prot_blocks, last_fill, memory_slots):
    vmem = pl.BlockSpec(memory_space=pltpu.VMEM)
    smem = pl.BlockSpec(memory_space=pltpu.SMEM)
    dma = pltpu.SemaphoreType.DMA
    row = jax.ShapeDtypeStruct((512, 1024), BF)

    def buf(*shape, dtype=BF):
        return pltpu.VMEM(shape, dtype)

    sems = [(3,), (PAIRS, 3), (PAIRS,), (PAIRS,), (PAIRS,)]
    sems += [(PAIRS,), (PAIRS, 3), (PAIRS, 3)]
    sems += [(PAIRS,)] + [(PAIRS, 3)] * 6 + [(PAIRS,)]
    square = (1024, 1024)
    outs = pl.pallas_call(
        kernel,
        out_shape=[row, row, row, jax.ShapeDtypeStruct(square, BF)],
        in_specs=[vmem] * 6 + [smem] * 3,
        out_specs=[vmem] * 4,
        scratch_shapes=[
            buf(PAIRS, 2, 1536, 128), buf(RING, 512 // QB, 2 * QB, BAND + 512),
            buf(RING, 512 // QB, 2 * QB, 1, dtype=F32), buf(RING, 512 // QB, 2 * QB, 1, dtype=F32),
            buf(8, 1536, dtype=F32), buf(16, 512), buf(128, 1536, dtype=F32), buf(128, 1536, dtype=F32),
            buf(512, 128), buf(PAIRS, 512, 128), buf(512, 128, dtype=F32), buf(PAIRS, 2, 512, 128, dtype=F32),
            buf(PAIRS, 2, 512, 128), buf(PAIRS, 2, 512, 128),
            buf(PAIRS, 2, 512, 128), buf(PAIRS, 2, 256, 128), buf(PAIRS, 2, 256, 128), buf(PAIRS, 3, 2, 64, 128),
            buf(PAIRS, 2, 64, 128), buf(PAIRS, 3, 2, 16, 128),
            buf(PAIRS, 2, 128, 512), buf(PAIRS, 128, 512), buf(PAIRS, 128, 512), buf(PAIRS, 3, 32, 512),
            buf(PAIRS, 4, 32, 128), buf(PAIRS, 3, 32, 128), buf(PAIRS, 32, 128, dtype=F32),
            buf(PAIRS, 3, 8, 128, dtype=F32), buf(PAIRS, 32, 128, dtype=F32), buf(PAIRS, 4, 32, 128),
            buf(PAIRS, 2, 128, 512),
        ]
        + [dma(s) for s in sems for _ in range(2)],
        compiler_params=pltpu.CompilerParams(
            collective_id=0, has_side_effects=True, vmem_limit_bytes=62 * 2**20
        ),
        name="fused",
    )(
        queries[0], key_rows[0], value_rows[0], cotangent[0], out_weight, memory_slots,
        memory_slots, prot_blocks, last_fill,
    )
    blocks = [pl.BlockSpec((128, 1024), lambda i: (i, 0))] * 3 + [pl.BlockSpec((256, 1024), lambda i: (i, 0))]
    dq, dk, dv, weight = pl.pallas_call(
        handed_on,
        grid=(4,),
        out_shape=[row, row, row, jax.ShapeDtypeStruct(square, F32)],
        in_specs=blocks,
        out_specs=blocks,
        compiler_params=pltpu.CompilerParams(vmem_limit_bytes=16 * 2**20),
        name="handed_on",
    )(*outs)
    return dq[None], dk[None], dv[None], weight


def solution(mesh):
    row = P("fam", "ctx", None)
    fam = P("fam", None)
    return jax.shard_map(
        per_device,
        mesh=mesh,
        in_specs=(row, row, row, row, P(), fam, fam, fam),
        out_specs=(row, row, row, P()),
        check_vma=False,
    )
```

```python
import jax
import jax.numpy as jnp
from jax import lax
from jax.experimental import pallas as pl
from jax.experimental.pallas import tpu as pltpu
from jax.sharding import PartitionSpec as P

F32 = jnp.float32
BF = jnp.bfloat16
NEG = -1e30
QB = 256
BAND = 512 + QB
PAIRS = 8
LEAD = 4
RING = LEAD + 1
KEEP = 3
MESH = pl.DeviceIdType.MESH


def nt(a, b):
    return lax.dot_general(a, b, (((1,), (1,)), ((), ())), preferred_element_type=F32)


def nn(a, b):
    return lax.dot_general(a, b, (((1,), (0,)), ((), ())), preferred_element_type=F32)


def tn(a, b):
    return lax.dot_general(a, b, (((0,), (0,)), ((), ())), preferred_element_type=F32)


def cols(p):
    return pl.ds(pl.multiple_of(p * 128, 128), 128)


def part(index, size):
    return pl.ds(pl.multiple_of(index * size, size), size)


def kernel(
    q_ref, k_ref, v_ref, cot_ref, w_ref, slots_ref, slot_ref, blocks_ref, fill_ref,
    dq_ref, dk_ref, dv_ref, wg_ref,
    kv, ebuf, stat, bias, pick_ref, dkt, dvt, att, do_all, vcol, own,
    bsend, brecv, mg, srecv, xs, xrecv, ys, yrecv,
    wb, w1, ws2, w2, ws3, w3, ws4, w4, f5, f6, f7,
    agy_s, agy_r, agx_s, agx_r, ags_s, ags_r, hal_s, hal_r, bak_s, bak_r,
    ms_s, ms_r, mx_s, mx_r, my_s, my_r,
    s1_s, s1_r, s2_s, s2_r, s3_s, s3_r, s4_s, s4_r, s5_s, s5_r, s6_s, s6_r, s7_s, s7_r, s8_s, s8_r,
):
    z = lax.axis_index("fam")
    me = lax.axis_index("ctx")
    x = me // 8
    y = (me // 2) % 4
    core = me % 2

    def at(xx, yy, cc):
        return (z, xx * 8 + yy * 2 + cc)

    sib = at(x, y, 1 - core)
    nxt = (z, (me + 1) % 32)
    prv = (z, (me + 31) % 32)
    across = (z, (me + 31 + 2 * core) % 32)
    ypeer = [at(x, (y + d) % 4, core) for d in (1, 2, 3)]
    xpeer = [at((x + d) % 4, y, core) for d in (1, 2, 3)]
    zpeer = [((z + d) % 4, me) for d in (1, 2, 3)]

    def rc(src, dst, send, recv, device):
        return pltpu.make_async_remote_copy(
            src_ref=src, dst_ref=dst, send_sem=send, recv_sem=recv, device_id=device, device_id_type=MESH
        )

    def ag_y():
        ref = kv.at[:, :, part(64 + core * 16 + x * 4 + y, 16)]
        return [rc(ref, ref, agy_s.at[d], agy_r.at[d], ypeer[d]) for d in range(3)]

    def ag_x(p):
        ref = kv.at[p, :, part(16 + core * 4 + x, 64)]
        return [rc(ref, ref, agx_s.at[p, d], agx_r.at[p, d], xpeer[d]) for d in range(3)]

    def ag_s(p):
        ref = kv.at[p, :, part(4 + core, 256)]
        return [rc(ref, ref, ags_s.at[p], ags_r.at[p], sib)]

    def halo_fwd(p):
        return [rc(kv.at[p, :, 512:1024], kv.at[p, :, 0:512], hal_s.at[p], hal_r.at[p], nxt)]

    def halo_back(p):
        return [rc(bsend.at[p], brecv.at[p], bak_s.at[p], bak_r.at[p], prv)]

    def mem_s(p):
        return [rc(mg.at[p, :, part(1 - core, 256)], srecv.at[p], ms_s.at[p], ms_r.at[p], sib)]

    def mem_x(p):
        return [
            rc(xs.at[p, :, part((x + 3 - d) % 4, 64)], xrecv.at[p, d], mx_s.at[p, d], mx_r.at[p, d], xpeer[2 - d])
            for d in range(3)
        ]

    def mem_y(p):
        return [
            rc(ys.at[p, :, part((y + d + 1) % 4, 16)], yrecv.at[p, d], my_s.at[p, d], my_r.at[p, d], ypeer[d])
            for d in range(3)
        ]

    def wt1(p):
        return [rc(wb.at[p, 1 - core], w1.at[p], s1_s.at[p], s1_r.at[p], sib)]

    def wt2(p):
        return [
            rc(ws2.at[p, part((z + d + 1) % 4, 32)], w2.at[p, d], s2_s.at[p, d], s2_r.at[p, d], zpeer[d])
            for d in range(3)
        ]

    def wt3(p):
        return [
            rc(ws3.at[p, (y + d + 1) % 4], w3.at[p, d], s3_s.at[p, d], s3_r.at[p, d], ypeer[d])
            for d in range(3)
        ]

    def wt4(p):
        return [
            rc(ws4.at[p, part((x + d + 1) % 4, 8)], w4.at[p, d], s4_s.at[p, d], s4_r.at[p, d], xpeer[d])
            for d in range(3)
        ]

    def wt5(p):
        ref = f5.at[p, part(x, 8)]
        return [rc(ref, ref, s5_s.at[p, d], s5_r.at[p, d], xpeer[d]) for d in range(3)]

    def wt6(p):
        ref = f6.at[p, y]
        return [rc(ref, ref, s6_s.at[p, d], s6_r.at[p, d], ypeer[d]) for d in range(3)]

    def wt7(p):
        ref = f7.at[p, core, part(z, 32)]
        return [rc(ref, ref, s7_s.at[p, d], s7_r.at[p, d], zpeer[d]) for d in range(3)]

    def wt8(p):
        return [rc(f7.at[p, core], f7.at[p, core], s8_s.at[p], s8_r.at[p], sib)]

    def start(copies):
        for c in copies:
            c.start()

    def wait(copies):
        for c in copies:
            c.wait()

    def start_up(copies):
        for d, c in enumerate(copies):
            pl.when(x + d + 1 < 4)(c.start)

    def wait_up(copies):
        for d, c in enumerate(copies):
            pl.when(x + d + 1 < 4)(c.wait_send)
            pl.when(x >= d + 1)(c.wait_recv)

    def start_down(copies):
        for d, c in enumerate(copies):
            pl.when(x >= d + 1)(c.start)

    def wait_down(copies):
        for d, c in enumerate(copies):
            pl.when(x >= d + 1)(c.wait_send)
            pl.when(x + d + 1 < 4)(c.wait_recv)

    def start_fwd(p):
        pl.when(me < 31)(halo_fwd(p)[0].start)

    def wait_fwd(p):
        pl.when(me < 31)(halo_fwd(p)[0].wait_send)
        pl.when(me > 0)(halo_fwd(p)[0].wait_recv)

    def start_back(p):
        pl.when(me > 0)(halo_back(p)[0].start)

    def wait_back(p):
        pl.when(me > 0)(halo_back(p)[0].wait_send)
        pl.when(me < 31)(halo_back(p)[0].wait_recv)

    for p in range(PAIRS):
        kv[p, :, 0:512, :] = jnp.zeros((2, 512, 128), BF)
        kv[p, :, 1024:1536, :] = jnp.zeros((2, 512, 128), BF)
        xrecv[p] = jnp.zeros((3, 2, 64, 128), BF)

    @pl.when(me == 31)
    def _():
        for p in range(PAIRS):
            brecv[p] = jnp.zeros((2, 512, 128), BF)

    barrier = pltpu.get_barrier_semaphore()
    for device in [sib, across] + ypeer + xpeer + zpeer:
        pl.semaphore_signal(barrier, inc=1, device_id=device, device_id_type=MESH)
    wide = lax.broadcasted_iota(jnp.int32, (16, 512), 1)
    line = lax.broadcasted_iota(jnp.int32, (16, 512), 0)
    chosen = jnp.zeros((16, 512), jnp.int32)
    for i in range(16):
        chosen = jnp.where(line == i, slot_ref[0, me * 16 + i], chosen)
    pick = jnp.where(wide == chosen, 1.0, 0.0).astype(BF)
    pick_ref[...] = pick
    mine = part(64 + core * 16 + x * 4 + y, 16)
    for i, r in enumerate((k_ref, v_ref)):
        for p in range(PAIRS):
            kv[p, i, 512:1024, :] = r[:, p * 128 : p * 128 + 128]
            kv[p, i, mine, :] = nn(pick, r[:, p * 128 : p * 128 + 128]).astype(BF)
    pl.semaphore_wait(barrier, 11)
    start(ag_y())
    start_fwd(0)
    start_fwd(1)

    here = lax.broadcasted_iota(jnp.int32, (512, 512), 1)
    there = lax.broadcasted_iota(jnp.int32, (512, 512), 0)
    origin = ((here // 16) % 16) * 32 + (here // 256) * 16 + here % 16
    move = jnp.where(there == origin, 1.0, 0.0).astype(BF)
    slots = jnp.broadcast_to(slots_ref[...], (16, 512))
    halves = nn((slots // 2).astype(F32).astype(BF), move)
    odds = nn((slots % 2).astype(F32).astype(BF), move)
    slots = (halves * 2.0 + odds).astype(jnp.int32)[:1]

    pos_band = me * 512 - 512 + lax.broadcasted_iota(jnp.int32, (1, 1024), 1)
    order = lax.broadcasted_iota(jnp.int32, (1, 512), 1) // 16
    holder = (order % 16) * 2 + order // 16
    pos = jnp.concatenate([pos_band, holder * 512 + slots], axis=1)
    block = (pos + 512) // 128 - 4
    prot = jnp.zeros((1, 1536), jnp.int32)
    limit = jnp.zeros((1, 1536), jnp.int32)
    first = jnp.int32(0)
    for i in range(32):
        end = first + blocks_ref[0, i]
        inside = (block >= first) & (block < end)
        prot = jnp.where(inside, i, prot)
        limit = jnp.where(inside, (end - 1) * 128 + fill_ref[0, i], limit)
        first = end
    real = (pos >= 0) & (pos < limit)
    is_mem = lax.broadcasted_iota(jnp.int32, (1, 1536), 1) >= 1024
    rows8 = lax.broadcasted_iota(jnp.int32, (8, 1536), 0)
    table = jnp.where(rows8 == 4, jnp.where(real, 1.0, 0.0), 0.0)
    for a in range(4):
        mine_prot = prot[:, 512 + a * 128 : 513 + a * 128]
        seen = real & ((is_mem & (prot < mine_prot)) | (jnp.logical_not(is_mem) & (prot == mine_prot)))
        table = jnp.where(rows8 == a, jnp.where(seen, 0.0, NEG), table)
    bias[...] = table
    vcol[...] = jnp.concatenate([table[:, 512:1024], jnp.zeros((120, 512), F32)], axis=0).T

    wait(ag_y())
    start_up(ag_x(0))
    start_up(ag_x(1))
    wait_up(ag_x(0))
    start(ag_s(0))

    lo = lax.broadcasted_iota(jnp.int32, (QB, 128), 1) < 64
    zero = jnp.zeros((QB, 128), BF)
    memory = slice(1024, 1536)

    def stacked(pair):
        return jnp.concatenate([jnp.where(lo, pair, zero), jnp.where(lo, zero, pair)], 0)

    def forward(p):
        slot = p % RING
        do_all[p] = nt(cot_ref[...], w_ref[part(p, 128), :]).astype(BF)
        rr = lax.broadcasted_iota(jnp.int32, (128, QB), 0)
        cc = lax.broadcasted_iota(jnp.int32, (128, QB), 1)
        for b in range(512 // QB):
            rows = slice(b * QB, (b + 1) * QB)
            band = slice(b * QB, b * QB + BAND)
            qs = stacked(q_ref[rows, cols(p)] * jnp.asarray(0.125, BF))
            sb = nt(qs, kv[p, 0, band, :])
            sm = nt(qs, kv[p, 0, memory, :])
            sums = []
            exps = []
            for g in range(2 * QB // 128):
                sub = g % (QB // 128)
                a = b * QB // 128 + sub
                group = slice(g * 128, g * 128 + 128)
                s = sb[group] + bias[a : a + 1, band]
                far = jnp.where(cc > rr + sub * 128, s[:, :QB], NEG)
                near = jnp.where(cc <= rr + sub * 128, s[:, 512:], NEG)
                s = jnp.concatenate([far, s[:, QB:512], near, sm[group] + bias[a : a + 1, memory]], 1)
                e = jnp.exp(s - jnp.max(s, axis=1, keepdims=True))
                sums.append(jnp.sum(e, axis=1, keepdims=True))
                exps.append(e.astype(BF))
            e = jnp.concatenate(exps, 0)
            ebuf[slot, b] = e
            o = nn(e[:, :BAND], kv[p, 1, band, :]) + nn(e[:, BAND:], kv[p, 1, memory, :])
            live = vcol[rows, 4:5]
            inv = jnp.concatenate([live, live], 0) / jnp.maximum(jnp.concatenate(sums, 0), 1.0)
            a = o * inv
            stat[slot, b, :, 0:1] = inv
            stat[slot, b, :, 1:2] = jnp.sum(a * stacked(do_all[p, rows, :]).astype(F32), axis=1, keepdims=True)
            att[rows, :] = jnp.where(lo, a[:QB], a[QB:]).astype(BF)
        for h in range(2):
            wb[p, h] = tn(att[...], cot_ref[:, h * 512 : h * 512 + 512]).astype(BF)

    def backward(p):
        slot = p % RING
        dkt[...] = jnp.zeros_like(dkt)
        dvt[...] = jnp.zeros_like(dvt)
        for b in range(512 // QB):
            rows = slice(b * QB, (b + 1) * QB)
            band = slice(b * QB, b * QB + BAND)
            inv = stat[slot, b, :, 0:1]
            rd = stat[slot, b, :, 1:2]
            dos = stacked(do_all[p, rows, :])
            eb = ebuf[slot, b, :, :BAND]
            em = ebuf[slot, b, :, BAND:]
            dsb = (eb.astype(F32) * (nt(dos, kv[p, 1, band, :]) - rd)).astype(BF)
            dsm = (em.astype(F32) * (nt(dos, kv[p, 1, memory, :]) - rd)).astype(BF)
            dqs = (nn(dsb, kv[p, 0, band, :]) + nn(dsm, kv[p, 0, memory, :])) * (inv * 0.125)
            dq_ref[rows, cols(p)] = jnp.where(lo, dqs[:QB], dqs[QB:]).astype(BF)
            qs = stacked(q_ref[rows, cols(p)] * jnp.asarray(0.125, BF))
            qn = (qs.astype(F32) * inv).astype(BF)
            don = (dos.astype(F32) * inv).astype(BF)
            dkt[:, band] += tn(qn, dsb)
            dkt[:, memory] += tn(qn, dsm)
            dvt[:, band] += tn(don, eb)
            dvt[:, memory] += tn(don, em)
        for i, t in enumerate((dkt, dvt)):
            mg[p, i] = t[:, 1024:].T.astype(BF)
            bsend[p, i] = t[:, :512].T.astype(BF)
            own[p % KEEP, i] = t[:, 512:1024].T

    def mem_sum_s(p):
        wait(mem_s(p))
        both = mg[p, :, part(core, 256), :].astype(F32) + srecv[p].astype(F32)
        xs[p] = both.astype(BF)
        start_down(mem_x(p))

    def mem_sum_x(p):
        wait_down(mem_x(p))
        total = xs[p, :, part(x, 64), :].astype(F32)
        for d in range(3):
            total += xrecv[p, d].astype(F32)
        ys[p] = total.astype(BF)
        start(mem_y(p))

    def mem_sum_y(p):
        wait(mem_y(p))
        wait_back(p)
        total = ys[p, :, part(y, 16), :].astype(F32)
        for d in range(3):
            total += yrecv[p, d].astype(F32)
        high = total.astype(BF)
        low = (total - high.astype(F32)).astype(BF)
        for i, ref in enumerate((dk_ref, dv_ref)):
            grad = own[p % KEEP, i] + brecv[p, i].astype(F32)
            grad += tn(pick_ref[...], high[i]) + tn(pick_ref[...], low[i])
            ref[:, cols(p)] = grad.astype(BF)

    def w_sum1(p):
        wait(wt1(p))
        ws2[p] = (wb[p, core].astype(F32) + w1[p].astype(F32)).astype(BF)
        start(wt2(p))

    def w_sum2(p):
        wait(wt2(p))
        total = ws2[p, part(z, 32), :].astype(F32)
        for d in range(3):
            total += w2[p, d].astype(F32)
        for c in range(4):
            ws3[p, c] = total[:, c * 128 : c * 128 + 128].astype(BF)
        start(wt3(p))

    def w_sum3(p):
        wait(wt3(p))
        total = ws3[p, y].astype(F32)
        for d in range(3):
            total += w3[p, d].astype(F32)
        ws4[p] = total
        start(wt4(p))

    def w_sum4(p):
        wait(wt4(p))
        total = ws4[p, part(x, 8), :]
        for d in range(3):
            total += w4[p, d]
        f5[p, part(x, 8), :] = total * (65536.0 ** -0.5)
        start(wt5(p))

    def w_put5(p):
        wait(wt5(p))
        f6[p, y] = f5[p].astype(BF)
        start(wt6(p))

    def w_put6(p):
        wait(wt6(p))
        for c in range(4):
            f7[p, core, part(z, 32), c * 128 : c * 128 + 128] = f6[p, c]
        start(wt7(p))

    def w_put7(p):
        wait(wt7(p))
        start(wt8(p))

    def w_put8(p):
        wait(wt8(p))
        rows = part(p, 128)
        for h in range(2):
            wg_ref[rows, h * 512 : h * 512 + 512] = f7[p, h]

    between = [(LEAD + 1, mem_sum_s), (7, w_put8)]
    after = [
        (LEAD + 1, mem_sum_x), (0, w_sum1), (1, w_sum2), (2, w_sum3), (3, w_sum4), (4, w_put5), (5, w_put6), (6, w_put7),
        (LEAD + 2, mem_sum_y),
    ]

    def run(t, stages):
        for lag, stage in stages:

            @pl.when((t >= lag) & (t < PAIRS + lag))
            def _(lag=lag, stage=stage):
                stage(t - lag)

    def step(t, carry):
        @pl.when(t < PAIRS - 2)
        def _():
            start_up(ag_x(t + 2))
            start_fwd(t + 2)

        @pl.when(t < PAIRS - 1)
        def _():
            wait_up(ag_x(t + 1))
            start(ag_s(t + 1))

        @pl.when(t < PAIRS)
        def _():
            wait(ag_s(t))
            wait_fwd(t)
            forward(t)
            start(wt1(t))

        run(t, between)

        @pl.when((t >= LEAD) & (t < PAIRS + LEAD))
        def _():
            backward(t - LEAD)
            start(mem_s(t - LEAD))
            start_back(t - LEAD)

        run(t, after)
        return carry

    lax.fori_loop(0, PAIRS + max(LEAD + 2, 7), step, 0)


def handed_on(*refs):
    for source, target in zip(refs[:4], refs[4:]):
        target[...] = source[...].astype(target.dtype)


def per_device(queries, key_rows, value_rows, cotangent, out_weight, prot_blocks, last_fill, memory_slots):
    vmem = pl.BlockSpec(memory_space=pltpu.VMEM)
    smem = pl.BlockSpec(memory_space=pltpu.SMEM)
    dma = pltpu.SemaphoreType.DMA
    row = jax.ShapeDtypeStruct((512, 1024), BF)

    def buf(*shape, dtype=BF):
        return pltpu.VMEM(shape, dtype)

    sems = [(3,), (PAIRS, 3), (PAIRS,), (PAIRS,), (PAIRS,)]
    sems += [(PAIRS,), (PAIRS, 3), (PAIRS, 3)]
    sems += [(PAIRS,)] + [(PAIRS, 3)] * 6 + [(PAIRS,)]
    square = (1024, 1024)
    outs = pl.pallas_call(
        kernel,
        out_shape=[row, row, row, jax.ShapeDtypeStruct(square, BF)],
        in_specs=[vmem] * 6 + [smem] * 3,
        out_specs=[vmem] * 4,
        scratch_shapes=[
            buf(PAIRS, 2, 1536, 128), buf(RING, 512 // QB, 2 * QB, BAND + 512),
            buf(RING, 512 // QB, 2 * QB, 128, dtype=F32),
            buf(8, 1536, dtype=F32), buf(16, 512), buf(128, 1536, dtype=F32), buf(128, 1536, dtype=F32),
            buf(512, 128), buf(PAIRS, 512, 128), buf(512, 128, dtype=F32), buf(KEEP, 2, 512, 128, dtype=F32),
            buf(PAIRS, 2, 512, 128), buf(PAIRS, 2, 512, 128),
            buf(PAIRS, 2, 512, 128), buf(PAIRS, 2, 256, 128), buf(PAIRS, 2, 256, 128), buf(PAIRS, 3, 2, 64, 128),
            buf(PAIRS, 2, 64, 128), buf(PAIRS, 3, 2, 16, 128),
            buf(PAIRS, 2, 128, 512), buf(PAIRS, 128, 512), buf(PAIRS, 128, 512), buf(PAIRS, 3, 32, 512),
            buf(PAIRS, 4, 32, 128), buf(PAIRS, 3, 32, 128), buf(PAIRS, 32, 128, dtype=F32),
            buf(PAIRS, 3, 8, 128, dtype=F32), buf(PAIRS, 32, 128, dtype=F32), buf(PAIRS, 4, 32, 128),
            buf(PAIRS, 2, 128, 512),
        ]
        + [dma(s) for s in sems for _ in range(2)],
        compiler_params=pltpu.CompilerParams(
            collective_id=0, has_side_effects=True, vmem_limit_bytes=62 * 2**20
        ),
        name="fused",
    )(
        queries[0], key_rows[0], value_rows[0], cotangent[0], out_weight, memory_slots,
        memory_slots, prot_blocks, last_fill,
    )
    blocks = [pl.BlockSpec((128, 1024), lambda i: (i, 0))] * 3 + [pl.BlockSpec((256, 1024), lambda i: (i, 0))]
    dq, dk, dv, weight = pl.pallas_call(
        handed_on,
        grid=(4,),
        out_shape=[row, row, row, jax.ShapeDtypeStruct(square, F32)],
        in_specs=blocks,
        out_specs=blocks,
        compiler_params=pltpu.CompilerParams(vmem_limit_bytes=60 * 2**20),
        name="handed_on",
    )(*outs)
    return dq[None], dk[None], dv[None], weight


def solution(mesh):
    row = P("fam", "ctx", None)
    fam = P("fam", None)
    return jax.shard_map(
        per_device,
        mesh=mesh,
        in_specs=(row, row, row, row, P(), fam, fam, fam),
        out_specs=(row, row, row, P()),
        check_vma=False,
    )
```

```python
import jax
import jax.numpy as jnp
from jax import lax
from jax.experimental import pallas as pl
from jax.experimental.pallas import tpu as pltpu
from jax.sharding import PartitionSpec as P

F32 = jnp.float32
BF = jnp.bfloat16
NEG = -1e30
QB = 256
BAND = 512 + QB
PAIRS = 8
LEAD = 2
RING = LEAD + 1
KEEP = 3
MESH = pl.DeviceIdType.MESH


def nt(a, b):
    return lax.dot_general(a, b, (((1,), (1,)), ((), ())), preferred_element_type=F32)


def nn(a, b):
    return lax.dot_general(a, b, (((1,), (0,)), ((), ())), preferred_element_type=F32)


def tn(a, b):
    return lax.dot_general(a, b, (((0,), (0,)), ((), ())), preferred_element_type=F32)


def cols(p):
    return pl.ds(pl.multiple_of(p * 128, 128), 128)


def part(index, size):
    return pl.ds(pl.multiple_of(index * size, size), size)


def kernel(
    q_ref, k_ref, v_ref, cot_ref, w_ref, slots_ref, slot_ref, blocks_ref, fill_ref,
    dq_ref, dk_ref, dv_ref, wg_ref,
    kv, ebuf, stat, bias, pick_ref, dkt, dvt, att, do_all, vcol, own,
    bsend, brecv, mg, srecv, xs, xrecv, ys, yrecv,
    wb, w1, ws2, w2, ws3, w3, ws4, w4, f5, f6, f7,
    agy_s, agy_r, agx_s, agx_r, ags_s, ags_r, hal_s, hal_r, bak_s, bak_r,
    ms_s, ms_r, mx_s, mx_r, my_s, my_r,
    s1_s, s1_r, s2_s, s2_r, s3_s, s3_r, s4_s, s4_r, s5_s, s5_r, s6_s, s6_r, s7_s, s7_r, s8_s, s8_r,
):
    z = lax.axis_index("fam")
    me = lax.axis_index("ctx")
    x = me // 8
    y = (me // 2) % 4
    core = me % 2

    def at(xx, yy, cc):
        return (z, xx * 8 + yy * 2 + cc)

    sib = at(x, y, 1 - core)
    nxt = (z, (me + 1) % 32)
    prv = (z, (me + 31) % 32)
    across = (z, (me + 31 + 2 * core) % 32)
    ypeer = [at(x, (y + d) % 4, core) for d in (1, 2, 3)]
    xpeer = [at((x + d) % 4, y, core) for d in (1, 2, 3)]
    zpeer = [((z + d) % 4, me) for d in (1, 2, 3)]

    def rc(src, dst, send, recv, device):
        return pltpu.make_async_remote_copy(
            src_ref=src, dst_ref=dst, send_sem=send, recv_sem=recv, device_id=device, device_id_type=MESH
        )

    def ag_y():
        ref = kv.at[:, :, part(64 + core * 16 + x * 4 + y, 16)]
        return [rc(ref, ref, agy_s.at[d], agy_r.at[d], ypeer[d]) for d in range(3)]

    def ag_x(p):
        ref = kv.at[p, :, part(16 + core * 4 + x, 64)]
        return [rc(ref, ref, agx_s.at[p, d], agx_r.at[p, d], xpeer[d]) for d in range(3)]

    def ag_s(p):
        ref = kv.at[p, :, part(4 + core, 256)]
        return [rc(ref, ref, ags_s.at[p], ags_r.at[p], sib)]

    def halo_fwd(p):
        return [rc(kv.at[p, :, 512:1024], kv.at[p, :, 0:512], hal_s.at[p], hal_r.at[p], nxt)]

    def halo_back(p):
        return [rc(bsend.at[p], brecv.at[p], bak_s.at[p], bak_r.at[p], prv)]

    def mem_s(p):
        return [rc(mg.at[p, :, part(1 - core, 256)], srecv.at[p], ms_s.at[p], ms_r.at[p], sib)]

    def mem_x(p):
        return [
            rc(xs.at[p, :, part((x + 3 - d) % 4, 64)], xrecv.at[p, d], mx_s.at[p, d], mx_r.at[p, d], xpeer[2 - d])
            for d in range(3)
        ]

    def mem_y(p):
        return [
            rc(ys.at[p, :, part((y + d + 1) % 4, 16)], yrecv.at[p, d], my_s.at[p, d], my_r.at[p, d], ypeer[d])
            for d in range(3)
        ]

    def wt1(p):
        return [rc(wb.at[p, 1 - core], w1.at[p], s1_s.at[p], s1_r.at[p], sib)]

    def wt2(p):
        return [
            rc(ws2.at[p, part((z + d + 1) % 4, 32)], w2.at[p, d], s2_s.at[p, d], s2_r.at[p, d], zpeer[d])
            for d in range(3)
        ]

    def wt3(p):
        return [
            rc(ws3.at[p, (y + d + 1) % 4], w3.at[p, d], s3_s.at[p, d], s3_r.at[p, d], ypeer[d])
            for d in range(3)
        ]

    def wt4(p):
        return [
            rc(ws4.at[p, part((x + d + 1) % 4, 8)], w4.at[p, d], s4_s.at[p, d], s4_r.at[p, d], xpeer[d])
            for d in range(3)
        ]

    def wt5(p):
        ref = f5.at[p, part(x, 8)]
        return [rc(ref, ref, s5_s.at[p, d], s5_r.at[p, d], xpeer[d]) for d in range(3)]

    def wt6(p):
        ref = f6.at[p, y]
        return [rc(ref, ref, s6_s.at[p, d], s6_r.at[p, d], ypeer[d]) for d in range(3)]

    def wt7(p):
        ref = f7.at[p, core, part(z, 32)]
        return [rc(ref, ref, s7_s.at[p, d], s7_r.at[p, d], zpeer[d]) for d in range(3)]

    def wt8(p):
        return [rc(f7.at[p, core], f7.at[p, core], s8_s.at[p], s8_r.at[p], sib)]

    def start(copies):
        for c in copies:
            c.start()

    def wait(copies):
        for c in copies:
            c.wait()

    def start_up(copies):
        for d, c in enumerate(copies):
            pl.when(x + d + 1 < 4)(c.start)

    def wait_up(copies):
        for d, c in enumerate(copies):
            pl.when(x + d + 1 < 4)(c.wait_send)
            pl.when(x >= d + 1)(c.wait_recv)

    def start_down(copies):
        for d, c in enumerate(copies):
            pl.when(x >= d + 1)(c.start)

    def wait_down(copies):
        for d, c in enumerate(copies):
            pl.when(x >= d + 1)(c.wait_send)
            pl.when(x + d + 1 < 4)(c.wait_recv)

    def start_fwd(p):
        pl.when(me < 31)(halo_fwd(p)[0].start)

    def wait_fwd(p):
        pl.when(me < 31)(halo_fwd(p)[0].wait_send)
        pl.when(me > 0)(halo_fwd(p)[0].wait_recv)

    def start_back(p):
        pl.when(me > 0)(halo_back(p)[0].start)

    def wait_back(p):
        pl.when(me > 0)(halo_back(p)[0].wait_send)
        pl.when(me < 31)(halo_back(p)[0].wait_recv)

    for p in range(PAIRS):
        kv[p, :, 1024:1536, :] = jnp.zeros((2, 512, 128), BF)
        xrecv[p] = jnp.zeros((3, 2, 64, 128), BF)

    @pl.when(me == 0)
    def _():
        for p in range(PAIRS):
            kv[p, :, 0:512, :] = jnp.zeros((2, 512, 128), BF)

    @pl.when(me == 31)
    def _():
        for p in range(PAIRS):
            brecv[p] = jnp.zeros((2, 512, 128), BF)

    barrier = pltpu.get_barrier_semaphore()
    for device in [sib, across] + ypeer + xpeer + zpeer:
        pl.semaphore_signal(barrier, inc=1, device_id=device, device_id_type=MESH)
    wide = lax.broadcasted_iota(jnp.int32, (16, 512), 1)
    line = lax.broadcasted_iota(jnp.int32, (16, 512), 0)
    chosen = jnp.zeros((16, 512), jnp.int32)
    for i in range(16):
        chosen = jnp.where(line == i, slot_ref[0, me * 16 + i], chosen)
    pick = jnp.where(wide == chosen, 1.0, 0.0).astype(BF)
    pick_ref[...] = pick
    mine = part(64 + core * 16 + x * 4 + y, 16)
    for i, r in enumerate((k_ref, v_ref)):
        chosen_rows = nn(pick, r[...]).astype(BF)
        for p in range(PAIRS):
            kv[p, i, mine, :] = chosen_rows[:, p * 128 : p * 128 + 128]
    pl.semaphore_wait(barrier, 11)
    start(ag_y())
    for i, r in enumerate((k_ref, v_ref)):
        for p in range(PAIRS):
            kv[p, i, 512:1024, :] = r[:, p * 128 : p * 128 + 128]
    start_fwd(0)
    start_fwd(1)

    here = lax.broadcasted_iota(jnp.int32, (512, 512), 1)
    there = lax.broadcasted_iota(jnp.int32, (512, 512), 0)
    origin = ((here // 16) % 16) * 32 + (here // 256) * 16 + here % 16
    move = jnp.where(there == origin, 1.0, 0.0).astype(BF)
    slots = jnp.broadcast_to(slots_ref[...], (16, 512))
    halves = nn((slots // 2).astype(F32).astype(BF), move)
    odds = nn((slots % 2).astype(F32).astype(BF), move)
    slots = (halves * 2.0 + odds).astype(jnp.int32)[:1]

    pos_band = me * 512 - 512 + lax.broadcasted_iota(jnp.int32, (1, 1024), 1)
    order = lax.broadcasted_iota(jnp.int32, (1, 512), 1) // 16
    holder = (order % 16) * 2 + order // 16
    pos = jnp.concatenate([pos_band, holder * 512 + slots], axis=1)
    block = (pos + 512) // 128 - 4
    prot = jnp.zeros((1, 1536), jnp.int32)
    limit = jnp.zeros((1, 1536), jnp.int32)
    first = jnp.int32(0)
    for i in range(32):
        end = first + blocks_ref[0, i]
        inside = (block >= first) & (block < end)
        prot = jnp.where(inside, i, prot)
        limit = jnp.where(inside, (end - 1) * 128 + fill_ref[0, i], limit)
        first = end
    real = (pos >= 0) & (pos < limit)
    is_mem = lax.broadcasted_iota(jnp.int32, (1, 1536), 1) >= 1024
    rows8 = lax.broadcasted_iota(jnp.int32, (8, 1536), 0)
    table = jnp.where(rows8 == 4, jnp.where(real, 1.0, 0.0), 0.0)
    for a in range(4):
        mine_prot = prot[:, 512 + a * 128 : 513 + a * 128]
        seen = real & ((is_mem & (prot < mine_prot)) | (jnp.logical_not(is_mem) & (prot == mine_prot)))
        table = jnp.where(rows8 == a, jnp.where(seen, 0.0, NEG), table)
    bias[...] = table
    vcol[...] = jnp.concatenate([table[:, 512:1024], jnp.zeros((120, 512), F32)], axis=0).T

    wait(ag_y())
    start_up(ag_x(0))
    start_up(ag_x(1))
    for p in range(PAIRS):
        do_all[p] = nt(cot_ref[...], w_ref[p * 128 : p * 128 + 128, :]).astype(BF)
    wait_up(ag_x(0))
    start(ag_s(0))

    lo = lax.broadcasted_iota(jnp.int32, (QB, 128), 1) < 64
    zero = jnp.zeros((QB, 128), BF)
    memory = slice(1024, 1536)

    def stacked(pair):
        return jnp.concatenate([jnp.where(lo, pair, zero), jnp.where(lo, zero, pair)], 0)

    def forward(p):
        slot = p % RING
        rr = lax.broadcasted_iota(jnp.int32, (128, QB), 0)
        cc = lax.broadcasted_iota(jnp.int32, (128, QB), 1)
        for b in range(512 // QB):
            rows = slice(b * QB, (b + 1) * QB)
            band = slice(b * QB, b * QB + BAND)
            qs = stacked(q_ref[rows, cols(p)] * jnp.asarray(0.125, BF))
            sb = nt(qs, kv[p, 0, band, :])
            sm = nt(qs, kv[p, 0, memory, :])
            sums = []
            exps = []
            for g in range(2 * QB // 128):
                sub = g % (QB // 128)
                a = b * QB // 128 + sub
                group = slice(g * 128, g * 128 + 128)
                s = sb[group] + bias[a : a + 1, band]
                far = jnp.where(cc > rr + sub * 128, s[:, :QB], NEG)
                near = jnp.where(cc <= rr + sub * 128, s[:, 512:], NEG)
                s = jnp.concatenate([far, s[:, QB:512], near, sm[group] + bias[a : a + 1, memory]], 1)
                e = jnp.exp(s - jnp.max(s, axis=1, keepdims=True))
                sums.append(jnp.sum(e, axis=1, keepdims=True))
                exps.append(e.astype(BF))
            e = jnp.concatenate(exps, 0)
            ebuf[slot, b] = e
            o = nn(e[:, :BAND], kv[p, 1, band, :]) + nn(e[:, BAND:], kv[p, 1, memory, :])
            live = vcol[rows, 4:5]
            inv = jnp.concatenate([live, live], 0) / jnp.maximum(jnp.concatenate(sums, 0), 1.0)
            a = o * inv
            stat[slot, b, :, 0:1] = inv
            stat[slot, b, :, 1:2] = jnp.sum(a * stacked(do_all[p, rows, :]).astype(F32), axis=1, keepdims=True)
            att[rows, :] = jnp.where(lo, a[:QB], a[QB:]).astype(BF)
        for h in range(2):
            wb[p, h] = tn(att[...], cot_ref[:, h * 512 : h * 512 + 512]).astype(BF)

    def backward(p):
        slot = p % RING
        dkt[...] = jnp.zeros_like(dkt)
        dvt[...] = jnp.zeros_like(dvt)
        for b in range(512 // QB):
            rows = slice(b * QB, (b + 1) * QB)
            band = slice(b * QB, b * QB + BAND)
            inv = stat[slot, b, :, 0:1]
            rd = stat[slot, b, :, 1:2]
            dos = stacked(do_all[p, rows, :])
            eb = ebuf[slot, b, :, :BAND]
            em = ebuf[slot, b, :, BAND:]
            dsb = (eb.astype(F32) * (nt(dos, kv[p, 1, band, :]) - rd)).astype(BF)
            dsm = (em.astype(F32) * (nt(dos, kv[p, 1, memory, :]) - rd)).astype(BF)
            dqs = (nn(dsb, kv[p, 0, band, :]) + nn(dsm, kv[p, 0, memory, :])) * (inv * 0.125)
            dq_ref[rows, cols(p)] = jnp.where(lo, dqs[:QB], dqs[QB:]).astype(BF)
            qs = stacked(q_ref[rows, cols(p)] * jnp.asarray(0.125, BF))
            qn = (qs.astype(F32) * inv).astype(BF)
            don = (dos.astype(F32) * inv).astype(BF)
            dkt[:, band] += tn(qn, dsb)
            dkt[:, memory] += tn(qn, dsm)
            dvt[:, band] += tn(don, eb)
            dvt[:, memory] += tn(don, em)
        for i, t in enumerate((dkt, dvt)):
            mg[p, i] = t[:, 1024:].T.astype(BF)
            bsend[p, i] = t[:, :512].T.astype(BF)
            own[p % KEEP, i] = t[:, 512:1024].T

    def mem_sum_s(p):
        wait(mem_s(p))
        both = mg[p, :, part(core, 256), :].astype(F32) + srecv[p].astype(F32)
        xs[p] = both.astype(BF)
        start_down(mem_x(p))

    def mem_sum_x(p):
        wait_down(mem_x(p))
        total = xs[p, :, part(x, 64), :].astype(F32)
        for d in range(3):
            total += xrecv[p, d].astype(F32)
        ys[p] = total.astype(BF)
        start(mem_y(p))

    def mem_sum_y(p):
        wait(mem_y(p))
        wait_back(p)
        total = ys[p, :, part(y, 16), :].astype(F32)
        for d in range(3):
            total += yrecv[p, d].astype(F32)
        high = total.astype(BF)
        low = (total - high.astype(F32)).astype(BF)
        for i, ref in enumerate((dk_ref, dv_ref)):
            grad = own[p % KEEP, i] + brecv[p, i].astype(F32)
            grad += tn(pick_ref[...], high[i]) + tn(pick_ref[...], low[i])
            ref[:, cols(p)] = grad.astype(BF)

    def w_sum1(p):
        wait(wt1(p))
        ws2[p] = (wb[p, core].astype(F32) + w1[p].astype(F32)).astype(BF)
        start(wt2(p))

    def w_sum2(p):
        wait(wt2(p))
        total = ws2[p, part(z, 32), :].astype(F32)
        for d in range(3):
            total += w2[p, d].astype(F32)
        for c in range(4):
            ws3[p, c] = total[:, c * 128 : c * 128 + 128].astype(BF)
        start(wt3(p))

    def w_sum3(p):
        wait(wt3(p))
        total = ws3[p, y].astype(F32)
        for d in range(3):
            total += w3[p, d].astype(F32)
        ws4[p] = total
        start(wt4(p))

    def w_sum4(p):
        wait(wt4(p))
        total = ws4[p, part(x, 8), :]
        for d in range(3):
            total += w4[p, d]
        f5[p, part(x, 8), :] = total * (65536.0 ** -0.5)
        start(wt5(p))

    def w_put5(p):
        wait(wt5(p))
        f6[p, y] = f5[p].astype(BF)
        start(wt6(p))

    def w_put6(p):
        wait(wt6(p))
        for c in range(4):
            f7[p, core, part(z, 32), c * 128 : c * 128 + 128] = f6[p, c]
        start(wt7(p))

    def w_put7(p):
        wait(wt7(p))
        start(wt8(p))

    def w_put8(p):
        wait(wt8(p))
        rows = part(p, 128)
        for h in range(2):
            wg_ref[rows, h * 512 : h * 512 + 512] = f7[p, h]

    between = [(LEAD + 1, mem_sum_s), (7, w_put8)]
    after = [
        (LEAD + 1, mem_sum_x), (0, w_sum1), (1, w_sum2), (2, w_sum3), (3, w_sum4), (4, w_put5), (5, w_put6), (6, w_put7),
        (LEAD + 2, mem_sum_y),
    ]

    def run(t, stages):
        for lag, stage in stages:

            @pl.when((t >= lag) & (t < PAIRS + lag))
            def _(lag=lag, stage=stage):
                stage(t - lag)

    def step(t, carry):
        @pl.when(t < PAIRS - 2)
        def _():
            start_up(ag_x(t + 2))
            start_fwd(t + 2)

        @pl.when(t < PAIRS - 1)
        def _():
            wait_up(ag_x(t + 1))
            start(ag_s(t + 1))

        @pl.when(t < PAIRS)
        def _():
            wait(ag_s(t))
            wait_fwd(t)
            forward(t)
            start(wt1(t))

        run(t, between)

        @pl.when((t >= LEAD) & (t < PAIRS + LEAD))
        def _():
            backward(t - LEAD)
            start(mem_s(t - LEAD))
            start_back(t - LEAD)

        run(t, after)
        return carry

    lax.fori_loop(0, PAIRS + max(LEAD + 2, 7), step, 0)


def handed_on(*refs):
    for source, target in zip(refs[:4], refs[4:]):
        target[...] = source[...].astype(target.dtype)


def per_device(queries, key_rows, value_rows, cotangent, out_weight, prot_blocks, last_fill, memory_slots):
    vmem = pl.BlockSpec(memory_space=pltpu.VMEM)
    smem = pl.BlockSpec(memory_space=pltpu.SMEM)
    dma = pltpu.SemaphoreType.DMA
    row = jax.ShapeDtypeStruct((512, 1024), BF)

    def buf(*shape, dtype=BF):
        return pltpu.VMEM(shape, dtype)

    sems = [(3,), (PAIRS, 3), (PAIRS,), (PAIRS,), (PAIRS,)]
    sems += [(PAIRS,), (PAIRS, 3), (PAIRS, 3)]
    sems += [(PAIRS,)] + [(PAIRS, 3)] * 6 + [(PAIRS,)]
    square = (1024, 1024)
    outs = pl.pallas_call(
        kernel,
        out_shape=[row, row, row, jax.ShapeDtypeStruct(square, BF)],
        in_specs=[vmem] * 6 + [smem] * 3,
        out_specs=[vmem] * 4,
        scratch_shapes=[
            buf(PAIRS, 2, 1536, 128), buf(RING, 512 // QB, 2 * QB, BAND + 512),
            buf(RING, 512 // QB, 2 * QB, 128, dtype=F32),
            buf(8, 1536, dtype=F32), buf(16, 512), buf(128, 1536, dtype=F32), buf(128, 1536, dtype=F32),
            buf(512, 128), buf(PAIRS, 512, 128), buf(512, 128, dtype=F32), buf(KEEP, 2, 512, 128, dtype=F32),
            buf(PAIRS, 2, 512, 128), buf(PAIRS, 2, 512, 128),
            buf(PAIRS, 2, 512, 128), buf(PAIRS, 2, 256, 128), buf(PAIRS, 2, 256, 128), buf(PAIRS, 3, 2, 64, 128),
            buf(PAIRS, 2, 64, 128), buf(PAIRS, 3, 2, 16, 128),
            buf(PAIRS, 2, 128, 512), buf(PAIRS, 128, 512), buf(PAIRS, 128, 512), buf(PAIRS, 3, 32, 512),
            buf(PAIRS, 4, 32, 128), buf(PAIRS, 3, 32, 128), buf(PAIRS, 32, 128, dtype=F32),
            buf(PAIRS, 3, 8, 128, dtype=F32), buf(PAIRS, 32, 128, dtype=F32), buf(PAIRS, 4, 32, 128),
            buf(PAIRS, 2, 128, 512),
        ]
        + [dma(s) for s in sems for _ in range(2)],
        compiler_params=pltpu.CompilerParams(
            collective_id=0, has_side_effects=True, vmem_limit_bytes=62 * 2**20
        ),
        name="fused",
    )(
        queries[0], key_rows[0], value_rows[0], cotangent[0], out_weight, memory_slots,
        memory_slots, prot_blocks, last_fill,
    )
    blocks = [pl.BlockSpec((128, 1024), lambda i: (i, 0))] * 3 + [pl.BlockSpec((256, 1024), lambda i: (i, 0))]
    dq, dk, dv, weight = pl.pallas_call(
        handed_on,
        grid=(4,),
        out_shape=[row, row, row, jax.ShapeDtypeStruct(square, F32)],
        in_specs=blocks,
        out_specs=blocks,
        compiler_params=pltpu.CompilerParams(vmem_limit_bytes=60 * 2**20),
        name="handed_on",
    )(*outs)
    return dq[None], dk[None], dv[None], weight


def solution(mesh):
    row = P("fam", "ctx", None)
    fam = P("fam", None)
    return jax.shard_map(
        per_device,
        mesh=mesh,
        in_specs=(row, row, row, row, P(), fam, fam, fam),
        out_specs=(row, row, row, P()),
        check_vma=False,
    )
```

```python
import jax
import jax.numpy as jnp
from jax import lax
from jax.experimental import pallas as pl
from jax.experimental.pallas import tpu as pltpu
from jax.sharding import PartitionSpec as P

F32 = jnp.float32
BF = jnp.bfloat16
NEG = -1e30
QB = 256
BAND = 512 + QB
PAIRS = 8
LEAD = 3
RING = LEAD + 1
KEEP = 3
MESH = pl.DeviceIdType.MESH


def nt(a, b):
    return lax.dot_general(a, b, (((1,), (1,)), ((), ())), preferred_element_type=F32)


def nn(a, b):
    return lax.dot_general(a, b, (((1,), (0,)), ((), ())), preferred_element_type=F32)


def tn(a, b):
    return lax.dot_general(a, b, (((0,), (0,)), ((), ())), preferred_element_type=F32)


def cols(p):
    return pl.ds(pl.multiple_of(p * 128, 128), 128)


def part(index, size):
    return pl.ds(pl.multiple_of(index * size, size), size)


def kernel(
    q_ref, k_ref, v_ref, cot_ref, w_ref, slots_ref, slot_ref, blocks_ref, fill_ref,
    dq_ref, dk_ref, dv_ref, wg_ref,
    kv, ebuf, stat, bias, pick_ref, dkt, dvt, att, do_all, vcol, own,
    bsend, brecv, mg, srecv, xs, xrecv, ys, yrecv,
    wb, w1, ws2, w2, ws3, w3, ws4, w4, f5, f6, f7,
    agy_s, agy_r, agx_s, agx_r, ags_s, ags_r, hal_s, hal_r, bak_s, bak_r,
    ms_s, ms_r, mx_s, mx_r, my_s, my_r,
    s1_s, s1_r, s2_s, s2_r, s3_s, s3_r, s4_s, s4_r, s5_s, s5_r, s6_s, s6_r, s7_s, s7_r, s8_s, s8_r,
):
    z = lax.axis_index("fam")
    me = lax.axis_index("ctx")
    x = me // 8
    y = (me // 2) % 4
    core = me % 2

    def at(xx, yy, cc):
        return (z, xx * 8 + yy * 2 + cc)

    sib = at(x, y, 1 - core)
    nxt = (z, (me + 1) % 32)
    prv = (z, (me + 31) % 32)
    across = (z, (me + 31 + 2 * core) % 32)
    ypeer = [at(x, (y + d) % 4, core) for d in (1, 2, 3)]
    xpeer = [at((x + d) % 4, y, core) for d in (1, 2, 3)]
    zpeer = [((z + d) % 4, me) for d in (1, 2, 3)]

    def rc(src, dst, send, recv, device):
        return pltpu.make_async_remote_copy(
            src_ref=src, dst_ref=dst, send_sem=send, recv_sem=recv, device_id=device, device_id_type=MESH
        )

    def ag_y():
        ref = kv.at[:, :, part(64 + core * 16 + x * 4 + y, 16)]
        return [rc(ref, ref, agy_s.at[d], agy_r.at[d], ypeer[d]) for d in range(3)]

    def ag_x(p):
        ref = kv.at[p, :, part(16 + core * 4 + x, 64)]
        return [rc(ref, ref, agx_s.at[p, d], agx_r.at[p, d], xpeer[d]) for d in range(3)]

    def ag_s(p):
        ref = kv.at[p, :, part(4 + core, 256)]
        return [rc(ref, ref, ags_s.at[p], ags_r.at[p], sib)]

    def halo_fwd(p):
        return [rc(kv.at[p, :, 512:1024], kv.at[p, :, 0:512], hal_s.at[p], hal_r.at[p], nxt)]

    def halo_back(p):
        return [rc(bsend.at[p], brecv.at[p], bak_s.at[p], bak_r.at[p], prv)]

    def mem_s(p):
        return [rc(mg.at[p, :, part(1 - core, 256)], srecv.at[p], ms_s.at[p], ms_r.at[p], sib)]

    def mem_x(p):
        return [
            rc(xs.at[p, :, part((x + 3 - d) % 4, 64)], xrecv.at[p, d], mx_s.at[p, d], mx_r.at[p, d], xpeer[2 - d])
            for d in range(3)
        ]

    def mem_y(p):
        return [
            rc(ys.at[p, :, part((y + d + 1) % 4, 16)], yrecv.at[p, d], my_s.at[p, d], my_r.at[p, d], ypeer[d])
            for d in range(3)
        ]

    def wt1(p):
        return [rc(wb.at[p, 1 - core], w1.at[p], s1_s.at[p], s1_r.at[p], sib)]

    def wt2(p):
        return [
            rc(ws2.at[p, part((z + d + 1) % 4, 32)], w2.at[p, d], s2_s.at[p, d], s2_r.at[p, d], zpeer[d])
            for d in range(3)
        ]

    def wt3(p):
        return [
            rc(ws3.at[p, (y + d + 1) % 4], w3.at[p, d], s3_s.at[p, d], s3_r.at[p, d], ypeer[d])
            for d in range(3)
        ]

    def wt4(p):
        return [
            rc(ws4.at[p, part((x + d + 1) % 4, 8)], w4.at[p, d], s4_s.at[p, d], s4_r.at[p, d], xpeer[d])
            for d in range(3)
        ]

    def wt5(p):
        ref = f5.at[p, part(x, 8)]
        return [rc(ref, ref, s5_s.at[p, d], s5_r.at[p, d], xpeer[d]) for d in range(3)]

    def wt6(p):
        ref = f6.at[p, y]
        return [rc(ref, ref, s6_s.at[p, d], s6_r.at[p, d], ypeer[d]) for d in range(3)]

    def wt7(p):
        ref = f7.at[p, core, part(z, 32)]
        return [rc(ref, ref, s7_s.at[p, d], s7_r.at[p, d], zpeer[d]) for d in range(3)]

    def wt8(p):
        return [rc(f7.at[p, core], f7.at[p, core], s8_s.at[p], s8_r.at[p], sib)]

    def start(copies):
        for c in copies:
            c.start()

    def wait(copies):
        for c in copies:
            c.wait()

    def start_up(copies):
        for d, c in enumerate(copies):
            pl.when(x + d + 1 < 4)(c.start)

    def wait_up(copies):
        for d, c in enumerate(copies):
            pl.when(x + d + 1 < 4)(c.wait_send)
            pl.when(x >= d + 1)(c.wait_recv)

    def start_down(copies):
        for d, c in enumerate(copies):
            pl.when(x >= d + 1)(c.start)

    def wait_down(copies):
        for d, c in enumerate(copies):
            pl.when(x >= d + 1)(c.wait_send)
            pl.when(x + d + 1 < 4)(c.wait_recv)

    def start_fwd(p):
        pl.when(me < 31)(halo_fwd(p)[0].start)

    def wait_fwd(p):
        pl.when(me < 31)(halo_fwd(p)[0].wait_send)
        pl.when(me > 0)(halo_fwd(p)[0].wait_recv)

    def start_back(p):
        pl.when(me > 0)(halo_back(p)[0].start)

    def wait_back(p):
        pl.when(me > 0)(halo_back(p)[0].wait_send)
        pl.when(me < 31)(halo_back(p)[0].wait_recv)

    for p in range(PAIRS):
        kv[p, :, 1024:1536, :] = jnp.zeros((2, 512, 128), BF)
        xrecv[p] = jnp.zeros((3, 2, 64, 128), BF)

    @pl.when(me == 0)
    def _():
        for p in range(PAIRS):
            kv[p, :, 0:512, :] = jnp.zeros((2, 512, 128), BF)

    @pl.when(me == 31)
    def _():
        for p in range(PAIRS):
            brecv[p] = jnp.zeros((2, 512, 128), BF)

    barrier = pltpu.get_barrier_semaphore()
    for device in [sib, across] + ypeer + xpeer + zpeer:
        pl.semaphore_signal(barrier, inc=1, device_id=device, device_id_type=MESH)
    wide = lax.broadcasted_iota(jnp.int32, (16, 512), 1)
    line = lax.broadcasted_iota(jnp.int32, (16, 512), 0)
    chosen = jnp.zeros((16, 512), jnp.int32)
    for i in range(16):
        chosen = jnp.where(line == i, slot_ref[0, me * 16 + i], chosen)
    pick = jnp.where(wide == chosen, 1.0, 0.0).astype(BF)
    pick_ref[...] = pick
    mine = part(64 + core * 16 + x * 4 + y, 16)
    for i, r in enumerate((k_ref, v_ref)):
        chosen_rows = nn(pick, r[...]).astype(BF)
        for p in range(PAIRS):
            kv[p, i, mine, :] = chosen_rows[:, p * 128 : p * 128 + 128]
    pl.semaphore_wait(barrier, 11)
    start(ag_y())
    for i, r in enumerate((k_ref, v_ref)):
        for p in range(PAIRS):
            kv[p, i, 512:1024, :] = r[:, p * 128 : p * 128 + 128]
    start_fwd(0)
    start_fwd(1)

    here = lax.broadcasted_iota(jnp.int32, (512, 512), 1)
    there = lax.broadcasted_iota(jnp.int32, (512, 512), 0)
    origin = ((here // 16) % 16) * 32 + (here // 256) * 16 + here % 16
    move = jnp.where(there == origin, 1.0, 0.0).astype(BF)
    slots = jnp.broadcast_to(slots_ref[...], (16, 512))
    halves = nn((slots // 2).astype(F32).astype(BF), move)
    odds = nn((slots % 2).astype(F32).astype(BF), move)
    slots = (halves * 2.0 + odds).astype(jnp.int32)[:1]

    pos_band = me * 512 - 512 + lax.broadcasted_iota(jnp.int32, (1, 1024), 1)
    order = lax.broadcasted_iota(jnp.int32, (1, 512), 1) // 16
    holder = (order % 16) * 2 + order // 16
    pos = jnp.concatenate([pos_band, holder * 512 + slots], axis=1)
    block = (pos + 512) // 128 - 4
    prot = jnp.zeros((1, 1536), jnp.int32)
    limit = jnp.zeros((1, 1536), jnp.int32)
    first = jnp.int32(0)
    for i in range(32):
        end = first + blocks_ref[0, i]
        inside = (block >= first) & (block < end)
        prot = jnp.where(inside, i, prot)
        limit = jnp.where(inside, (end - 1) * 128 + fill_ref[0, i], limit)
        first = end
    real = (pos >= 0) & (pos < limit)
    is_mem = lax.broadcasted_iota(jnp.int32, (1, 1536), 1) >= 1024
    rows8 = lax.broadcasted_iota(jnp.int32, (8, 1536), 0)
    table = jnp.where(rows8 == 4, jnp.where(real, 1.0, 0.0), 0.0)
    for a in range(4):
        mine_prot = prot[:, 512 + a * 128 : 513 + a * 128]
        seen = real & ((is_mem & (prot < mine_prot)) | (jnp.logical_not(is_mem) & (prot == mine_prot)))
        table = jnp.where(rows8 == a, jnp.where(seen, 0.0, NEG), table)
    bias[...] = table
    vcol[...] = jnp.concatenate([table[:, 512:1024], jnp.zeros((120, 512), F32)], axis=0).T

    wait(ag_y())
    start_up(ag_x(0))
    start_up(ag_x(1))
    for p in range(PAIRS):
        do_all[p] = nt(cot_ref[...], w_ref[p * 128 : p * 128 + 128, :]).astype(BF)
    wait_up(ag_x(0))
    start(ag_s(0))

    lo = lax.broadcasted_iota(jnp.int32, (QB, 128), 1) < 64
    zero = jnp.zeros((QB, 128), BF)
    memory = slice(1024, 1536)

    def stacked(pair):
        return jnp.concatenate([jnp.where(lo, pair, zero), jnp.where(lo, zero, pair)], 0)

    def forward(p):
        slot = p % RING
        rr = lax.broadcasted_iota(jnp.int32, (128, QB), 0)
        cc = lax.broadcasted_iota(jnp.int32, (128, QB), 1)
        for b in range(512 // QB):
            rows = slice(b * QB, (b + 1) * QB)
            band = slice(b * QB, b * QB + BAND)
            qs = stacked(q_ref[rows, cols(p)] * jnp.asarray(0.125, BF))
            sb = nt(qs, kv[p, 0, band, :])
            sm = nt(qs, kv[p, 0, memory, :])
            sums = []
            exps = []
            for g in range(2 * QB // 128):
                sub = g % (QB // 128)
                a = b * QB // 128 + sub
                group = slice(g * 128, g * 128 + 128)
                s = sb[group] + bias[a : a + 1, band]
                far = jnp.where(cc > rr + sub * 128, s[:, :QB], NEG)
                near = jnp.where(cc <= rr + sub * 128, s[:, 512:], NEG)
                s = jnp.concatenate([far, s[:, QB:512], near, sm[group] + bias[a : a + 1, memory]], 1)
                e = jnp.exp(s - jnp.max(s, axis=1, keepdims=True))
                sums.append(jnp.sum(e, axis=1, keepdims=True))
                exps.append(e.astype(BF))
            e = jnp.concatenate(exps, 0)
            ebuf[slot, b] = e
            o = nn(e[:, :BAND], kv[p, 1, band, :]) + nn(e[:, BAND:], kv[p, 1, memory, :])
            live = vcol[rows, 4:5]
            inv = jnp.concatenate([live, live], 0) / jnp.maximum(jnp.concatenate(sums, 0), 1.0)
            a = o * inv
            stat[slot, b, :, 0:1] = inv
            stat[slot, b, :, 1:2] = jnp.sum(a * stacked(do_all[p, rows, :]).astype(F32), axis=1, keepdims=True)
            att[rows, :] = jnp.where(lo, a[:QB], a[QB:]).astype(BF)
        for h in range(2):
            wb[p, h] = tn(att[...], cot_ref[:, h * 512 : h * 512 + 512]).astype(BF)

    def backward(p):
        slot = p % RING
        dkt[...] = jnp.zeros_like(dkt)
        dvt[...] = jnp.zeros_like(dvt)
        for b in range(512 // QB):
            rows = slice(b * QB, (b + 1) * QB)
            band = slice(b * QB, b * QB + BAND)
            inv = stat[slot, b, :, 0:1]
            rd = stat[slot, b, :, 1:2]
            dos = stacked(do_all[p, rows, :])
            eb = ebuf[slot, b, :, :BAND]
            em = ebuf[slot, b, :, BAND:]
            dsb = (eb.astype(F32) * (nt(dos, kv[p, 1, band, :]) - rd)).astype(BF)
            dsm = (em.astype(F32) * (nt(dos, kv[p, 1, memory, :]) - rd)).astype(BF)
            dqs = (nn(dsb, kv[p, 0, band, :]) + nn(dsm, kv[p, 0, memory, :])) * (inv * 0.125)
            dq_ref[rows, cols(p)] = jnp.where(lo, dqs[:QB], dqs[QB:]).astype(BF)
            qs = stacked(q_ref[rows, cols(p)] * jnp.asarray(0.125, BF))
            qn = (qs.astype(F32) * inv).astype(BF)
            don = (dos.astype(F32) * inv).astype(BF)
            dkt[:, band] += tn(qn, dsb)
            dkt[:, memory] += tn(qn, dsm)
            dvt[:, band] += tn(don, eb)
            dvt[:, memory] += tn(don, em)
        for i, t in enumerate((dkt, dvt)):
            mg[p, i] = t[:, 1024:].T.astype(BF)
            bsend[p, i] = t[:, :512].T.astype(BF)
            own[p % KEEP, i] = t[:, 512:1024].T

    def mem_sum_s(p):
        wait(mem_s(p))
        both = mg[p, :, part(core, 256), :].astype(F32) + srecv[p].astype(F32)
        xs[p] = both.astype(BF)
        start_down(mem_x(p))

    def mem_sum_x(p):
        wait_down(mem_x(p))
        total = xs[p, :, part(x, 64), :].astype(F32)
        for d in range(3):
            total += xrecv[p, d].astype(F32)
        ys[p] = total.astype(BF)
        start(mem_y(p))

    def mem_sum_y(p):
        wait(mem_y(p))
        wait_back(p)
        total = ys[p, :, part(y, 16), :].astype(F32)
        for d in range(3):
            total += yrecv[p, d].astype(F32)
        high = total.astype(BF)
        low = (total - high.astype(F32)).astype(BF)
        for i, ref in enumerate((dk_ref, dv_ref)):
            grad = own[p % KEEP, i] + brecv[p, i].astype(F32)
            grad += tn(pick_ref[...], high[i]) + tn(pick_ref[...], low[i])
            ref[:, cols(p)] = grad.astype(BF)

    def w_sum1(p):
        wait(wt1(p))
        ws2[p] = (wb[p, core].astype(F32) + w1[p].astype(F32)).astype(BF)
        start(wt2(p))

    def w_sum2(p):
        wait(wt2(p))
        total = ws2[p, part(z, 32), :].astype(F32)
        for d in range(3):
            total += w2[p, d].astype(F32)
        for c in range(4):
            ws3[p, c] = total[:, c * 128 : c * 128 + 128].astype(BF)
        start(wt3(p))

    def w_sum3(p):
        wait(wt3(p))
        total = ws3[p, y].astype(F32)
        for d in range(3):
            total += w3[p, d].astype(F32)
        ws4[p] = total
        start(wt4(p))

    def w_sum4(p):
        wait(wt4(p))
        total = ws4[p, part(x, 8), :]
        for d in range(3):
            total += w4[p, d]
        f5[p, part(x, 8), :] = total * (65536.0 ** -0.5)
        start(wt5(p))

    def w_put5(p):
        wait(wt5(p))
        f6[p, y] = f5[p].astype(BF)
        start(wt6(p))

    def w_put6(p):
        wait(wt6(p))
        for c in range(4):
            f7[p, core, part(z, 32), c * 128 : c * 128 + 128] = f6[p, c]
        start(wt7(p))

    def w_put7(p):
        wait(wt7(p))
        start(wt8(p))

    def w_put8(p):
        wait(wt8(p))
        rows = part(p, 128)
        for h in range(2):
            wg_ref[rows, h * 512 : h * 512 + 512] = f7[p, h]

    between = [(LEAD + 1, mem_sum_s), (7, w_put8)]
    after = [
        (LEAD + 1, mem_sum_x), (0, w_sum1), (1, w_sum2), (2, w_sum3), (3, w_sum4), (4, w_put5), (5, w_put6), (6, w_put7),
        (LEAD + 2, mem_sum_y),
    ]

    def run(t, stages):
        for lag, stage in stages:

            @pl.when((t >= lag) & (t < PAIRS + lag))
            def _(lag=lag, stage=stage):
                stage(t - lag)

    def step(t, carry):
        @pl.when(t < PAIRS - 2)
        def _():
            start_up(ag_x(t + 2))
            start_fwd(t + 2)

        @pl.when(t < PAIRS - 1)
        def _():
            wait_up(ag_x(t + 1))
            start(ag_s(t + 1))

        @pl.when(t < PAIRS)
        def _():
            wait(ag_s(t))
            wait_fwd(t)
            forward(t)
            start(wt1(t))

        run(t, between)

        @pl.when((t >= LEAD) & (t < PAIRS + LEAD))
        def _():
            backward(t - LEAD)
            start(mem_s(t - LEAD))
            start_back(t - LEAD)

        run(t, after)
        return carry

    lax.fori_loop(0, PAIRS + max(LEAD + 2, 7), step, 0)


def handed_on(*refs):
    for source, target in zip(refs[:4], refs[4:]):
        target[...] = source[...].astype(target.dtype)


def per_device(queries, key_rows, value_rows, cotangent, out_weight, prot_blocks, last_fill, memory_slots):
    vmem = pl.BlockSpec(memory_space=pltpu.VMEM)
    smem = pl.BlockSpec(memory_space=pltpu.SMEM)
    dma = pltpu.SemaphoreType.DMA
    row = jax.ShapeDtypeStruct((512, 1024), BF)

    def buf(*shape, dtype=BF):
        return pltpu.VMEM(shape, dtype)

    sems = [(3,), (PAIRS, 3), (PAIRS,), (PAIRS,), (PAIRS,)]
    sems += [(PAIRS,), (PAIRS, 3), (PAIRS, 3)]
    sems += [(PAIRS,)] + [(PAIRS, 3)] * 6 + [(PAIRS,)]
    square = (1024, 1024)
    outs = pl.pallas_call(
        kernel,
        out_shape=[row, row, row, jax.ShapeDtypeStruct(square, BF)],
        in_specs=[vmem] * 6 + [smem] * 3,
        out_specs=[vmem] * 4,
        scratch_shapes=[
            buf(PAIRS, 2, 1536, 128), buf(RING, 512 // QB, 2 * QB, BAND + 512),
            buf(RING, 512 // QB, 2 * QB, 128, dtype=F32),
            buf(8, 1536, dtype=F32), buf(16, 512), buf(128, 1536, dtype=F32), buf(128, 1536, dtype=F32),
            buf(512, 128), buf(PAIRS, 512, 128), buf(512, 128, dtype=F32), buf(KEEP, 2, 512, 128, dtype=F32),
            buf(PAIRS, 2, 512, 128), buf(PAIRS, 2, 512, 128),
            buf(PAIRS, 2, 512, 128), buf(PAIRS, 2, 256, 128), buf(PAIRS, 2, 256, 128), buf(PAIRS, 3, 2, 64, 128),
            buf(PAIRS, 2, 64, 128), buf(PAIRS, 3, 2, 16, 128),
            buf(PAIRS, 2, 128, 512), buf(PAIRS, 128, 512), buf(PAIRS, 128, 512), buf(PAIRS, 3, 32, 512),
            buf(PAIRS, 4, 32, 128), buf(PAIRS, 3, 32, 128), buf(PAIRS, 32, 128, dtype=F32),
            buf(PAIRS, 3, 8, 128, dtype=F32), buf(PAIRS, 32, 128, dtype=F32), buf(PAIRS, 4, 32, 128),
            buf(PAIRS, 2, 128, 512),
        ]
        + [dma(s) for s in sems for _ in range(2)],
        compiler_params=pltpu.CompilerParams(
            collective_id=0, has_side_effects=True, vmem_limit_bytes=62 * 2**20
        ),
        name="fused",
    )(
        queries[0], key_rows[0], value_rows[0], cotangent[0], out_weight, memory_slots,
        memory_slots, prot_blocks, last_fill,
    )
    blocks = [pl.BlockSpec((128, 1024), lambda i: (i, 0))] * 3 + [pl.BlockSpec((256, 1024), lambda i: (i, 0))]
    dq, dk, dv, weight = pl.pallas_call(
        handed_on,
        grid=(4,),
        out_shape=[row, row, row, jax.ShapeDtypeStruct(square, F32)],
        in_specs=blocks,
        out_specs=blocks,
        compiler_params=pltpu.CompilerParams(vmem_limit_bytes=60 * 2**20),
        name="handed_on",
    )(*outs)
    return dq[None], dk[None], dv[None], weight


def solution(mesh):
    row = P("fam", "ctx", None)
    fam = P("fam", None)
    return jax.shard_map(
        per_device,
        mesh=mesh,
        in_specs=(row, row, row, row, P(), fam, fam, fam),
        out_specs=(row, row, row, P()),
        check_vma=False,
    )
```

```python
import jax
import jax.numpy as jnp
from jax import lax
from jax.experimental import pallas as pl
from jax.experimental.pallas import tpu as pltpu
from jax.sharding import PartitionSpec as P

F32 = jnp.float32
BF = jnp.bfloat16
NEG = -1e30
QB = 256
BAND = 512 + QB
PAIRS = 8
LEAD = 3
RING = LEAD + 1
KEEP = 3
MESH = pl.DeviceIdType.MESH


def nt(a, b):
    return lax.dot_general(a, b, (((1,), (1,)), ((), ())), preferred_element_type=F32)


def nn(a, b):
    return lax.dot_general(a, b, (((1,), (0,)), ((), ())), preferred_element_type=F32)


def tn(a, b):
    return lax.dot_general(a, b, (((0,), (0,)), ((), ())), preferred_element_type=F32)


def cols(p):
    return pl.ds(pl.multiple_of(p * 128, 128), 128)


def part(index, size):
    return pl.ds(pl.multiple_of(index * size, size), size)


def kernel(
    q_ref, k_ref, v_ref, cot_ref, w_ref, slots_ref, slot_ref, blocks_ref, fill_ref,
    dq_ref, dk_ref, dv_ref, wg_ref,
    kv, ebuf, stat, bias, pick_ref, dkt, dvt, att, do_all, vcol, own,
    bsend, brecv, mg, srecv, xs, xrecv, ys, yrecv,
    wb, w1, ws2, w2, ws3, w3, ws4, w4, f5, f6, f7,
    agy_s, agy_r, agx_s, agx_r, ags_s, ags_r, hal_s, hal_r, bak_s, bak_r,
    ms_s, ms_r, mx_s, mx_r, my_s, my_r,
    s1_s, s1_r, s2_s, s2_r, s3_s, s3_r, s4_s, s4_r, s5_s, s5_r, s6_s, s6_r, s7_s, s7_r, s8_s, s8_r,
):
    z = lax.axis_index("fam")
    me = lax.axis_index("ctx")
    x = me // 8
    y = (me // 2) % 4
    core = me % 2

    def at(xx, yy, cc):
        return (z, xx * 8 + yy * 2 + cc)

    sib = at(x, y, 1 - core)
    nxt = (z, (me + 1) % 32)
    prv = (z, (me + 31) % 32)
    across = (z, (me + 31 + 2 * core) % 32)
    ypeer = [at(x, (y + d) % 4, core) for d in (1, 2, 3)]
    xpeer = [at((x + d) % 4, y, core) for d in (1, 2, 3)]
    zpeer = [((z + d) % 4, me) for d in (1, 2, 3)]

    def rc(src, dst, send, recv, device):
        return pltpu.make_async_remote_copy(
            src_ref=src, dst_ref=dst, send_sem=send, recv_sem=recv, device_id=device, device_id_type=MESH
        )

    def ag_y():
        ref = kv.at[:, :, part(64 + core * 16 + x * 4 + y, 16)]
        return [rc(ref, ref, agy_s.at[d], agy_r.at[d], ypeer[d]) for d in range(3)]

    def ag_x(p):
        ref = kv.at[p, :, part(16 + core * 4 + x, 64)]
        return [rc(ref, ref, agx_s.at[p, d], agx_r.at[p, d], xpeer[d]) for d in range(3)]

    def ag_s(p):
        ref = kv.at[p, :, part(4 + core, 256)]
        return [rc(ref, ref, ags_s.at[p], ags_r.at[p], sib)]

    def halo_fwd(p):
        return [rc(kv.at[p, :, 512:1024], kv.at[p, :, 0:512], hal_s.at[p], hal_r.at[p], nxt)]

    def halo_back(p):
        return [rc(bsend.at[p], brecv.at[p], bak_s.at[p], bak_r.at[p], prv)]

    def mem_s(p):
        return [rc(mg.at[p, :, part(1 - core, 256)], srecv.at[p], ms_s.at[p], ms_r.at[p], sib)]

    def mem_x(p):
        return [
            rc(xs.at[p, :, part((x + 3 - d) % 4, 64)], xrecv.at[p, d], mx_s.at[p, d], mx_r.at[p, d], xpeer[2 - d])
            for d in range(3)
        ]

    def mem_y(p):
        return [
            rc(ys.at[p, :, part((y + d + 1) % 4, 16)], yrecv.at[p, d], my_s.at[p, d], my_r.at[p, d], ypeer[d])
            for d in range(3)
        ]

    def wt1(p):
        return [rc(wb.at[p, 1 - core], w1.at[p], s1_s.at[p], s1_r.at[p], sib)]

    def wt2(p):
        return [
            rc(ws2.at[p, part((z + d + 1) % 4, 32)], w2.at[p, d], s2_s.at[p, d], s2_r.at[p, d], zpeer[d])
            for d in range(3)
        ]

    def wt3(p):
        return [
            rc(ws3.at[p, (y + d + 1) % 4], w3.at[p, d], s3_s.at[p, d], s3_r.at[p, d], ypeer[d])
            for d in range(3)
        ]

    def wt4(p):
        return [
            rc(ws4.at[p, part((x + d + 1) % 4, 8)], w4.at[p, d], s4_s.at[p, d], s4_r.at[p, d], xpeer[d])
            for d in range(3)
        ]

    def wt5(p):
        ref = f5.at[p, part(x, 8)]
        return [rc(ref, ref, s5_s.at[p, d], s5_r.at[p, d], xpeer[d]) for d in range(3)]

    def wt6(p):
        ref = f6.at[p, y]
        return [rc(ref, ref, s6_s.at[p, d], s6_r.at[p, d], ypeer[d]) for d in range(3)]

    def wt7(p):
        ref = f7.at[p, core, part(z, 32)]
        return [rc(ref, ref, s7_s.at[p, d], s7_r.at[p, d], zpeer[d]) for d in range(3)]

    def wt8(p):
        return [rc(f7.at[p, core], f7.at[p, core], s8_s.at[p], s8_r.at[p], sib)]

    def start(copies):
        for c in copies:
            c.start()

    def wait(copies):
        for c in copies:
            c.wait()

    def start_up(copies):
        for d, c in enumerate(copies):
            pl.when(x + d + 1 < 4)(c.start)

    def wait_up(copies):
        for d, c in enumerate(copies):
            pl.when(x + d + 1 < 4)(c.wait_send)
            pl.when(x >= d + 1)(c.wait_recv)

    def start_down(copies):
        for d, c in enumerate(copies):
            pl.when(x >= d + 1)(c.start)

    def wait_down(copies):
        for d, c in enumerate(copies):
            pl.when(x >= d + 1)(c.wait_send)
            pl.when(x + d + 1 < 4)(c.wait_recv)

    def start_fwd(p):
        pl.when(me < 31)(halo_fwd(p)[0].start)

    def wait_fwd(p):
        pl.when(me < 31)(halo_fwd(p)[0].wait_send)
        pl.when(me > 0)(halo_fwd(p)[0].wait_recv)

    def start_back(p):
        pl.when(me > 0)(halo_back(p)[0].start)

    def wait_back(p):
        pl.when(me > 0)(halo_back(p)[0].wait_send)
        pl.when(me < 31)(halo_back(p)[0].wait_recv)

    for p in range(PAIRS):
        kv[p, :, 1024:1536, :] = jnp.zeros((2, 512, 128), BF)
        xrecv[p] = jnp.zeros((3, 2, 64, 128), BF)

    @pl.when(me == 0)
    def _():
        for p in range(PAIRS):
            kv[p, :, 0:512, :] = jnp.zeros((2, 512, 128), BF)

    @pl.when(me == 31)
    def _():
        for p in range(PAIRS):
            brecv[p] = jnp.zeros((2, 512, 128), BF)

    barrier = pltpu.get_barrier_semaphore()
    for device in [sib, across] + ypeer + xpeer + zpeer:
        pl.semaphore_signal(barrier, inc=1, device_id=device, device_id_type=MESH)
    wide = lax.broadcasted_iota(jnp.int32, (16, 512), 1)
    line = lax.broadcasted_iota(jnp.int32, (16, 512), 0)
    chosen = jnp.zeros((16, 512), jnp.int32)
    for i in range(16):
        chosen = jnp.where(line == i, slot_ref[0, me * 16 + i], chosen)
    pick = jnp.where(wide == chosen, 1.0, 0.0).astype(BF)
    pick_ref[...] = pick
    mine = part(64 + core * 16 + x * 4 + y, 16)
    for i, r in enumerate((k_ref, v_ref)):
        chosen_rows = nn(pick, r[...]).astype(BF)
        for p in range(PAIRS):
            kv[p, i, mine, :] = chosen_rows[:, p * 128 : p * 128 + 128]
    pl.semaphore_wait(barrier, 11)
    start(ag_y())
    for i, r in enumerate((k_ref, v_ref)):
        for p in range(PAIRS):
            kv[p, i, 512:1024, :] = r[:, p * 128 : p * 128 + 128]
    start_fwd(0)
    start_fwd(1)

    here = lax.broadcasted_iota(jnp.int32, (512, 512), 1)
    there = lax.broadcasted_iota(jnp.int32, (512, 512), 0)
    origin = ((here // 16) % 16) * 32 + (here // 256) * 16 + here % 16
    move = jnp.where(there == origin, 1.0, 0.0).astype(BF)
    slots = jnp.broadcast_to(slots_ref[...], (16, 512))
    halves = nn((slots // 2).astype(F32).astype(BF), move)
    odds = nn((slots % 2).astype(F32).astype(BF), move)
    slots = (halves * 2.0 + odds).astype(jnp.int32)[:1]

    pos_band = me * 512 - 512 + lax.broadcasted_iota(jnp.int32, (1, 1024), 1)
    order = lax.broadcasted_iota(jnp.int32, (1, 512), 1) // 16
    holder = (order % 16) * 2 + order // 16
    pos = jnp.concatenate([pos_band, holder * 512 + slots], axis=1)
    block = (pos + 512) // 128 - 4
    prot = jnp.zeros((1, 1536), jnp.int32)
    limit = jnp.zeros((1, 1536), jnp.int32)
    first = jnp.int32(0)
    for i in range(32):
        end = first + blocks_ref[0, i]
        inside = (block >= first) & (block < end)
        prot = jnp.where(inside, i, prot)
        limit = jnp.where(inside, (end - 1) * 128 + fill_ref[0, i], limit)
        first = end
    real = (pos >= 0) & (pos < limit)
    is_mem = lax.broadcasted_iota(jnp.int32, (1, 1536), 1) >= 1024
    rows8 = lax.broadcasted_iota(jnp.int32, (8, 1536), 0)
    table = jnp.where(rows8 == 4, jnp.where(real, 1.0, 0.0), 0.0)
    for a in range(4):
        mine_prot = prot[:, 512 + a * 128 : 513 + a * 128]
        seen = real & ((is_mem & (prot < mine_prot)) | (jnp.logical_not(is_mem) & (prot == mine_prot)))
        table = jnp.where(rows8 == a, jnp.where(seen, 0.0, NEG), table)
    bias[...] = table
    vcol[...] = jnp.concatenate([table[:, 512:1024], jnp.zeros((120, 512), F32)], axis=0).T

    wait(ag_y())
    start_up(ag_x(0))
    start_up(ag_x(1))
    for p in range(PAIRS):
        do_all[p] = nt(cot_ref[...], w_ref[p * 128 : p * 128 + 128, :]).astype(BF)
    wait_up(ag_x(0))
    start(ag_s(0))

    lo = lax.broadcasted_iota(jnp.int32, (QB, 128), 1) < 64
    zero = jnp.zeros((QB, 128), BF)
    memory = slice(1024, 1536)

    def stacked(pair):
        return jnp.concatenate([jnp.where(lo, pair, zero), jnp.where(lo, zero, pair)], 0)

    def forward(p):
        slot = p % RING
        rr = lax.broadcasted_iota(jnp.int32, (128, QB), 0)
        cc = lax.broadcasted_iota(jnp.int32, (128, QB), 1)
        for b in range(512 // QB):
            rows = slice(b * QB, (b + 1) * QB)
            band = slice(b * QB, b * QB + BAND)
            qs = stacked(q_ref[rows, cols(p)] * jnp.asarray(0.125, BF))
            sb = nt(qs, kv[p, 0, band, :])
            sm = nt(qs, kv[p, 0, memory, :])
            sums = []
            exps = []
            for g in range(2 * QB // 128):
                sub = g % (QB // 128)
                a = b * QB // 128 + sub
                group = slice(g * 128, g * 128 + 128)
                s = sb[group] + bias[a : a + 1, band]
                far = jnp.where(cc > rr + sub * 128, s[:, :QB], NEG)
                near = jnp.where(cc <= rr + sub * 128, s[:, 512:], NEG)
                s = jnp.concatenate([far, s[:, QB:512], near, sm[group] + bias[a : a + 1, memory]], 1)
                e = jnp.exp(s - jnp.max(s, axis=1, keepdims=True))
                sums.append(jnp.sum(e, axis=1, keepdims=True))
                exps.append(e.astype(BF))
            e = jnp.concatenate(exps, 0)
            ebuf[slot, b] = e
            o = nn(e[:, :BAND], kv[p, 1, band, :]) + nn(e[:, BAND:], kv[p, 1, memory, :])
            live = vcol[rows, 4:5]
            inv = jnp.concatenate([live, live], 0) / jnp.maximum(jnp.concatenate(sums, 0), 1.0)
            a = o * inv
            stat[slot, b, :, 0:1] = inv
            stat[slot, b, :, 1:2] = jnp.sum(a * stacked(do_all[p, rows, :]).astype(F32), axis=1, keepdims=True)
            att[rows, :] = jnp.where(lo, a[:QB], a[QB:]).astype(BF)
        for h in range(2):
            wb[p, h] = tn(att[...], cot_ref[:, h * 512 : h * 512 + 512]).astype(BF)

    def backward(p):
        slot = p % RING
        dkt[...] = jnp.zeros_like(dkt)
        dvt[...] = jnp.zeros_like(dvt)
        for b in range(512 // QB):
            rows = slice(b * QB, (b + 1) * QB)
            band = slice(b * QB, b * QB + BAND)
            inv = stat[slot, b, :, 0:1]
            rd = stat[slot, b, :, 1:2]
            dos = stacked(do_all[p, rows, :])
            eb = ebuf[slot, b, :, :BAND]
            em = ebuf[slot, b, :, BAND:]
            dsb = (eb.astype(F32) * (nt(dos, kv[p, 1, band, :]) - rd)).astype(BF)
            dsm = (em.astype(F32) * (nt(dos, kv[p, 1, memory, :]) - rd)).astype(BF)
            dqs = (nn(dsb, kv[p, 0, band, :]) + nn(dsm, kv[p, 0, memory, :])) * (inv * 0.125)
            dq_ref[rows, cols(p)] = jnp.where(lo, dqs[:QB], dqs[QB:]).astype(BF)
            qs = stacked(q_ref[rows, cols(p)] * jnp.asarray(0.125, BF))
            qn = (qs.astype(F32) * inv).astype(BF)
            don = (dos.astype(F32) * inv).astype(BF)
            dkt[:, band] += tn(qn, dsb)
            dkt[:, memory] += tn(qn, dsm)
            dvt[:, band] += tn(don, eb)
            dvt[:, memory] += tn(don, em)
        for i, t in enumerate((dkt, dvt)):
            mg[p, i] = t[:, 1024:].T.astype(BF)
            bsend[p, i] = t[:, :512].T.astype(BF)
            own[p % KEEP, i] = t[:, 512:1024].T

    def mem_sum_s(p):
        wait(mem_s(p))
        both = mg[p, :, part(core, 256), :].astype(F32) + srecv[p].astype(F32)
        xs[p] = both.astype(BF)
        start_down(mem_x(p))

    def mem_sum_x(p):
        wait_down(mem_x(p))
        total = xs[p, :, part(x, 64), :].astype(F32)
        for d in range(3):
            total += xrecv[p, d].astype(F32)
        ys[p] = total.astype(BF)
        start(mem_y(p))

    def mem_sum_y(p):
        wait(mem_y(p))
        wait_back(p)
        total = ys[p, :, part(y, 16), :].astype(F32)
        for d in range(3):
            total += yrecv[p, d].astype(F32)
        high = total.astype(BF)
        low = (total - high.astype(F32)).astype(BF)
        for i, ref in enumerate((dk_ref, dv_ref)):
            grad = own[p % KEEP, i] + brecv[p, i].astype(F32)
            grad += tn(pick_ref[...], high[i]) + tn(pick_ref[...], low[i])
            ref[:, cols(p)] = grad.astype(BF)

    def w_sum1(p):
        wait(wt1(p))
        ws2[p] = (wb[p, core].astype(F32) + w1[p].astype(F32)).astype(BF)
        start(wt2(p))

    def w_sum2(p):
        wait(wt2(p))
        total = ws2[p, part(z, 32), :].astype(F32)
        for d in range(3):
            total += w2[p, d].astype(F32)
        for c in range(4):
            ws3[p, c] = total[:, c * 128 : c * 128 + 128].astype(BF)
        start(wt3(p))

    def w_sum3(p):
        wait(wt3(p))
        total = ws3[p, y].astype(F32)
        for d in range(3):
            total += w3[p, d].astype(F32)
        ws4[p] = total
        start(wt4(p))

    def w_sum4(p):
        wait(wt4(p))
        total = ws4[p, part(x, 8), :]
        for d in range(3):
            total += w4[p, d]
        f5[p, part(x, 8), :] = total * (65536.0 ** -0.5)
        start(wt5(p))

    def w_put5(p):
        wait(wt5(p))
        f6[p, y] = f5[p].astype(BF)
        start(wt6(p))

    def w_put6(p):
        wait(wt6(p))
        for c in range(4):
            f7[p, core, part(z, 32), c * 128 : c * 128 + 128] = f6[p, c]
        start(wt7(p))

    def w_put7(p):
        wait(wt7(p))
        start(wt8(p))

    def w_put8(p):
        wait(wt8(p))
        rows = part(p, 128)
        for h in range(2):
            wg_ref[rows, h * 512 : h * 512 + 512] = f7[p, h]

    between = [(LEAD + 1, mem_sum_s), (7, w_put8)]
    after = [
        (LEAD + 1, mem_sum_x), (0, w_sum1), (1, w_sum2), (2, w_sum3), (3, w_sum4), (4, w_put5), (5, w_put6), (6, w_put7),
        (LEAD + 2, mem_sum_y),
    ]

    hurried = [w_sum1, w_sum2, w_sum3, w_sum4, w_put5, w_put6, w_put7, w_put8]

    def run(t, stages):
        for lag, stage in stages:

            early = stage in hurried
            last = PAIRS - 1 if early else PAIRS

            @pl.when((t >= lag) & (t < last + lag))
            def _(lag=lag, stage=stage):
                stage(t - lag)

            if early and lag > 0:

                @pl.when(t == last + lag - 1)
                def _(stage=stage):
                    stage(PAIRS - 1)

    def step(t, carry):
        @pl.when(t < PAIRS - 2)
        def _():
            start_up(ag_x(t + 2))
            start_fwd(t + 2)

        @pl.when(t < PAIRS - 1)
        def _():
            wait_up(ag_x(t + 1))
            start(ag_s(t + 1))

        @pl.when(t < PAIRS)
        def _():
            wait(ag_s(t))
            wait_fwd(t)
            forward(t)
            start(wt1(t))

        run(t, between)

        @pl.when(t == PAIRS - 1)
        def _():
            w_sum1(PAIRS - 1)

        @pl.when((t >= LEAD) & (t < PAIRS + LEAD))
        def _():
            backward(t - LEAD)
            start(mem_s(t - LEAD))
            start_back(t - LEAD)

        run(t, after)
        return carry

    lax.fori_loop(0, PAIRS + max(LEAD + 2, 6), step, 0)


def handed_on(*refs):
    for source, target in zip(refs[:4], refs[4:]):
        target[...] = source[...].astype(target.dtype)


def per_device(queries, key_rows, value_rows, cotangent, out_weight, prot_blocks, last_fill, memory_slots):
    vmem = pl.BlockSpec(memory_space=pltpu.VMEM)
    smem = pl.BlockSpec(memory_space=pltpu.SMEM)
    dma = pltpu.SemaphoreType.DMA
    row = jax.ShapeDtypeStruct((512, 1024), BF)

    def buf(*shape, dtype=BF):
        return pltpu.VMEM(shape, dtype)

    sems = [(3,), (PAIRS, 3), (PAIRS,), (PAIRS,), (PAIRS,)]
    sems += [(PAIRS,), (PAIRS, 3), (PAIRS, 3)]
    sems += [(PAIRS,)] + [(PAIRS, 3)] * 6 + [(PAIRS,)]
    square = (1024, 1024)
    outs = pl.pallas_call(
        kernel,
        out_shape=[row, row, row, jax.ShapeDtypeStruct(square, BF)],
        in_specs=[vmem] * 6 + [smem] * 3,
        out_specs=[vmem] * 4,
        scratch_shapes=[
            buf(PAIRS, 2, 1536, 128), buf(RING, 512 // QB, 2 * QB, BAND + 512),
            buf(RING, 512 // QB, 2 * QB, 128, dtype=F32),
            buf(8, 1536, dtype=F32), buf(16, 512), buf(128, 1536, dtype=F32), buf(128, 1536, dtype=F32),
            buf(512, 128), buf(PAIRS, 512, 128), buf(512, 128, dtype=F32), buf(KEEP, 2, 512, 128, dtype=F32),
            buf(PAIRS, 2, 512, 128), buf(PAIRS, 2, 512, 128),
            buf(PAIRS, 2, 512, 128), buf(PAIRS, 2, 256, 128), buf(PAIRS, 2, 256, 128), buf(PAIRS, 3, 2, 64, 128),
            buf(PAIRS, 2, 64, 128), buf(PAIRS, 3, 2, 16, 128),
            buf(PAIRS, 2, 128, 512), buf(PAIRS, 128, 512), buf(PAIRS, 128, 512), buf(PAIRS, 3, 32, 512),
            buf(PAIRS, 4, 32, 128), buf(PAIRS, 3, 32, 128), buf(PAIRS, 32, 128, dtype=F32),
            buf(PAIRS, 3, 8, 128, dtype=F32), buf(PAIRS, 32, 128, dtype=F32), buf(PAIRS, 4, 32, 128),
            buf(PAIRS, 2, 128, 512),
        ]
        + [dma(s) for s in sems for _ in range(2)],
        compiler_params=pltpu.CompilerParams(
            collective_id=0, has_side_effects=True, vmem_limit_bytes=62 * 2**20
        ),
        name="fused",
    )(
        queries[0], key_rows[0], value_rows[0], cotangent[0], out_weight, memory_slots,
        memory_slots, prot_blocks, last_fill,
    )
    blocks = [pl.BlockSpec((128, 1024), lambda i: (i, 0))] * 3 + [pl.BlockSpec((256, 1024), lambda i: (i, 0))]
    dq, dk, dv, weight = pl.pallas_call(
        handed_on,
        grid=(4,),
        out_shape=[row, row, row, jax.ShapeDtypeStruct(square, F32)],
        in_specs=blocks,
        out_specs=blocks,
        compiler_params=pltpu.CompilerParams(vmem_limit_bytes=60 * 2**20),
        name="handed_on",
    )(*outs)
    return dq[None], dk[None], dv[None], weight


def solution(mesh):
    row = P("fam", "ctx", None)
    fam = P("fam", None)
    return jax.shard_map(
        per_device,
        mesh=mesh,
        in_specs=(row, row, row, row, P(), fam, fam, fam),
        out_specs=(row, row, row, P()),
        check_vma=False,
    )
```
